256 devices in a mesh: context: 64 (over x, z_lo, y), tensor: 4 (over z_hi, core).
Axes of the slice: x: 4, y: 4, z: 8 (z_hi: 2, z_lo: 4; z = z_hi * 4 + z_lo), core: 2. Of those that a mesh axis runs over, the one named last changes fastest.
Arguments:
- queries: bfloat16 [16384, 4096], P('context', 'tensor'), may hold values from -6 to 6
- keys: bfloat16 [16384, 4096], P('context', 'tensor'), may hold values from -6 to 6
- values: bfloat16 [16384, 4096], P('context', 'tensor'), may hold values from -6 to 6
- cotangent: bfloat16 [16384, 4096], P('context', 'tensor'), may hold values from -6 to 6
- filter_param: bfloat16 [16384, 1024], P('context'), may hold values from -120 to 120
- skip: float32 [4096], P('tensor'), may hold values from 0.5 to 1.5
Outputs:
- output: bfloat16 [16384, 4096], P('context', 'tensor')
- d_queries: bfloat16 [16384, 4096], P('context', 'tensor')
- d_keys: bfloat16 [16384, 4096], P('context', 'tensor')
- d_values: bfloat16 [16384, 4096], P('context', 'tensor')
- filter_grad: float32 [16384, 1024], P(('context', 'tensor'))
The draws below stay inside these ranges and needn't reach their ends.
All inputs are finite; a program needn't handle non-finite values.
Results may differ from the reference program's by a relative error of at most 0.014.
Values may be sent and summed in bfloat16 or wider, within the bound.
A program may use at most 128 MiB of HBM per device.

```python
import math
import jax
import jax.numpy as jnp
from jax import lax

WIDTH = 4096
SEQ = 16384
FILTERS = 1024


def draw_filter_param(key, part):
    key = jax.random.fold_in(key, 11)
    rate_key, noise_key = jax.random.split(key)
    positions = jnp.arange(SEQ, dtype=jnp.float32)[:, None]
    shortest = SEQ / 400.0
    spans = jax.random.uniform(rate_key, (FILTERS,), jnp.float32, math.log(shortest), math.log(4.0 * SEQ))
    lifetime = jnp.exp(spans)
    decay = jnp.exp(-positions / lifetime)
    energy = (1.0 - jnp.exp(-2.0 * SEQ / lifetime)) / (1.0 - jnp.exp(-2.0 / lifetime))
    noise = jax.random.truncated_normal(noise_key, -4.0, 4.0, (SEQ, FILTERS), jnp.float32)
    return (noise * decay * jnp.sqrt(SEQ / energy)).astype(jnp.bfloat16)


def block_levels(rng, extent, shards, least, top_value):
    def one(position, shards_of):
        steps = jax.random.uniform(jax.random.fold_in(jax.random.fold_in(rng, 6), position), (shards_of,), jnp.float32, least / len(shards), top_value / len(shards))
        return jnp.repeat(jnp.exp(steps), extent[position] // shards_of).reshape((-1,) + (1,) * (len(extent) - position - 1))

    gain = one(*shards[0])
    for cut in shards[1:]:
        gain = gain * one(*cut)
    return gain


def scatter_about(rng, extent, spread, bound, cuts=(), kind=jnp.bfloat16):
    drawn = jax.random.normal(rng, extent, jnp.float32) * spread
    if len(cuts) > 0:
        drawn = block_levels(rng, extent, cuts, -0.22, 0.18) * drawn
    return jnp.clip(drawn, min=-bound, max=bound).astype(kind)


def setup_inputs(seed: int = 0) -> dict:
    key_list = jax.random.split(jax.random.key(seed), 7)
    queries = scatter_about(key_list[0], (SEQ, WIDTH), 1.0, 6.0, ((0, 64), (1, 4)))
    keys = scatter_about(key_list[1], (SEQ, WIDTH), 1.0, 6.0, ((0, 64), (1, 4)))
    values = scatter_about(key_list[2], (SEQ, WIDTH), 1.0, 6.0, ((0, 64), (1, 4)))
    cotangent = scatter_about(key_list[3], (SEQ, WIDTH), 1.0, 6.0, ((0, 64), (1, 4)))
    filter_param = draw_filter_param(jax.random.fold_in(key_list[6], 71), 0)
    skip = jnp.clip(0.5 + 1.0 * jax.random.uniform(key_list[5], (WIDTH,), jnp.float32) ** block_levels(key_list[5], (WIDTH,), ((0, 4),), -0.2, 0.2), 0.5, 1.5)
    return dict(queries=queries, keys=keys, values=values, cotangent=cotangent, filter_param=filter_param, skip=skip)


def reference(queries, keys, values, cotangent, filter_param, skip):
    seq_len = queries.shape[0]
    width = queries.shape[1]
    groups = filter_param.shape[1]
    scale = 1.0 / math.sqrt(seq_len)
    gated = (keys.astype(jnp.float32) * values.astype(jnp.float32)).astype(jnp.bfloat16)
    grad_in = (queries.astype(jnp.float32) * cotangent.astype(jnp.float32)).astype(jnp.bfloat16)
    block = min(128, groups)
    count = groups // block
    padded_len = 2 * seq_len

    def arrange(field):
        return field.astype(jnp.float32).reshape(seq_len, 4, count, block).transpose(2, 0, 1, 3)
    taps = (filter_param.astype(jnp.float32) * scale).reshape(seq_len, count, block).transpose(1, 0, 2)

    def per_block(items):
        gated_part, grad_part, taps_part = items
        gated_freq = jnp.fft.rfft(gated_part, n=padded_len, axis=0)
        grad_freq = jnp.fft.rfft(grad_part, n=padded_len, axis=0)
        taps_freq = jnp.fft.rfft(taps_part, n=padded_len, axis=0)[:, None, :]
        conv = jnp.fft.irfft(gated_freq * taps_freq, n=padded_len, axis=0)[:seq_len]
        back = jnp.fft.irfft(jnp.conj(taps_freq) * grad_freq, n=padded_len, axis=0)[:seq_len]
        corr = jnp.fft.irfft(jnp.conj(gated_freq) * grad_freq, n=padded_len, axis=0)[:seq_len]
        return (conv, back, lax.optimization_barrier(jnp.sum(corr, axis=1)) * scale)
    conv, back, filter_grad = lax.map(per_block, (arrange(gated), arrange(grad_in), taps))
    conv = conv.transpose(1, 2, 0, 3).reshape(seq_len, width).astype(jnp.bfloat16)
    back = back.transpose(1, 2, 0, 3).reshape(seq_len, width).astype(jnp.bfloat16)
    filter_grad = filter_grad.transpose(1, 0, 2).reshape(seq_len, groups)
    mixed = conv.astype(jnp.float32) + skip * gated.astype(jnp.float32)
    output = (queries.astype(jnp.float32) * mixed).astype(jnp.bfloat16)
    d_queries = (cotangent.astype(jnp.float32) * mixed).astype(jnp.bfloat16)
    d_gated = back.astype(jnp.float32) + skip * grad_in.astype(jnp.float32)
    d_keys = (d_gated * values.astype(jnp.float32)).astype(jnp.bfloat16)
    d_values = (d_gated * keys.astype(jnp.float32)).astype(jnp.bfloat16)
    return (output, d_queries, d_keys, d_values, filter_grad)
```

```python
import functools
import math

import jax
import jax.numpy as jnp
import ml_dtypes
import numpy as np
from jax import lax
from jax.experimental import pallas as pl
from jax.experimental.pallas import tpu as pltpu
from jax.sharding import PartitionSpec as P

MESH = pl.DeviceIdType.MESH
F32 = jnp.float32
BF16 = jnp.bfloat16


def make_tables(blocks, span):
    length = blocks * span
    row = np.arange(blocks, dtype=np.float64)
    col = np.arange(span, dtype=np.float64)
    outer = 2.0 * np.pi * np.outer(row + 0.25, row) / blocks
    twist = 2.0 * np.pi * np.outer(row + 0.25, col) / length
    inner = 2.0 * np.pi * (np.outer(col, col) % span) / span
    outer_fwd = np.concatenate([np.cos(outer), -np.sin(outer)], axis=0)
    outer_inv = np.concatenate([np.cos(outer).T, -np.sin(outer).T], axis=1)
    cos, sin = np.cos(inner), np.sin(inner)
    inner_fwd = np.block([[cos, -sin], [sin, cos]])
    inner_inv = np.block([[cos, sin], [-sin, cos]])
    half = ml_dtypes.bfloat16
    return (
        outer_fwd.astype(half),
        outer_inv.astype(half),
        np.cos(twist).astype(np.float32),
        (-np.sin(twist)).astype(np.float32),
        inner_fwd.astype(half),
        inner_inv.astype(half),
    )


def dot(a, b):
    return jnp.dot(a, b, preferred_element_type=F32)


def spread(turned, groups):
    rows, span = turned.shape
    part = rows // (2 * groups)
    first = turned[: rows // 2].reshape(groups, part, span)
    second = turned[rows // 2 :].reshape(groups, part, span)
    return jnp.concatenate([first, second], axis=1).astype(BF16)


def gather_rows(blocks):
    groups, rows, span = blocks.shape
    wide = blocks.astype(F32)
    first = wide[:, : rows // 2].reshape(groups * rows // 2, span)
    second = wide[:, rows // 2 :].reshape(groups * rows // 2, span)
    return jnp.concatenate([first, second], axis=0)


def fold(rows):
    half = rows.shape[2] // 2
    return jnp.concatenate([rows[:, :, :half], rows[:, :, half:]], axis=1).astype(BF16)


def unfold(rows):
    part = rows.shape[1] // 2
    wide = rows.astype(F32)
    return jnp.concatenate([wide[:, :part], wide[:, part:]], axis=2)


def kernel(
    groups,
    scale,
    q_ref, k_ref, v_ref, g_ref, f_ref, skip_ref,
    outer_fwd, outer_inv, twist_cos, twist_sin, inner_fwd, inner_inv,
    out_ref, dq_ref, dk_ref, dv_ref, df_ref,
    x_send, x_recv, g_send, g_recv, c_send, c_recv, b_send, b_recv,
    f_send, f_recv, f_other, r_mine, r_other, r_send, r_recv,
    h_send, h_recv, t_send, t_recv,
    time_buf, spec_x, spec_h, spec_g,
    send_sem, recv_sem,
):
    span = q_ref.shape[0]
    chans = x_send.shape[1]
    step = min(4, chans)
    me = lax.axis_index("context")
    mine = lax.axis_index("tensor")
    core = mine % 2
    upper = mine // 2
    sibling = mine + 1 - 2 * core
    across = mine + 2 - 4 * upper

    def start_all(src, dst, slot):
        def body(s, carry):
            to = (me + s) % groups
            pltpu.make_async_remote_copy(
                src_ref=src.at[to], dst_ref=dst.at[me],
                send_sem=send_sem.at[slot], recv_sem=recv_sem.at[slot],
                device_id={"context": to}, device_id_type=MESH,
            ).start()
            return carry
        lax.fori_loop(1, groups, body, 0)
        dst[pl.ds(me, 1)] = src[pl.ds(me, 1)]

    def all_of(src, dst, slot):
        return pltpu.make_async_remote_copy(
            src_ref=src.at[pl.ds(0, groups - 1)], dst_ref=dst.at[pl.ds(0, groups - 1)],
            send_sem=send_sem.at[slot], recv_sem=recv_sem.at[slot],
            device_id={"context": (me + 1) % groups}, device_id_type=MESH,
        )

    def one(src, dst, slot, to):
        return pltpu.make_async_remote_copy(
            src_ref=src, dst_ref=dst,
            send_sem=send_sem.at[slot], recv_sem=recv_sem.at[slot],
            device_id={"tensor": to}, device_id_type=MESH,
        )

    def fill(field):
        flat = field.reshape(groups * chans, span)
        time_buf[0] = flat[:, : span // 2]
        time_buf[1] = flat[:, span // 2 :]

    def filled():
        flat = jnp.concatenate([time_buf[0], time_buf[1]], axis=1)
        return flat.reshape(groups, chans, span)

    def forward(dst):
        def body(n, carry):
            parts = []
            for c in range(step):
                rows = pl.ds(n * step + c, groups, stride=chans)
                field = jnp.concatenate([time_buf[0, rows, :], time_buf[1, rows, :]], axis=1)
                field = field.astype(BF16)
                first = dot(outer_fwd[...], field)
                re, im = first[:groups], first[groups:]
                tc, ts = twist_cos[...], twist_sin[...]
                parts.append(
                    jnp.concatenate([re * tc - im * ts, re * ts + im * tc], axis=1).astype(BF16)
                )
            rows = jnp.concatenate(parts, axis=0)
            dst[pl.ds(pl.multiple_of(n * step * groups, step * groups), step * groups), :] = dot(
                rows, inner_fwd[...]
            )
            return carry
        lax.fori_loop(0, chans // step, body, 0)

    def inverse(a_ref, b_ref, conj):
        def body(n, carry):
            here = pl.ds(pl.multiple_of(n * step * groups, step * groups), step * groups)
            ar, ai = a_ref[here, :span], a_ref[here, span:]
            br, bi = b_ref[here, :span], b_ref[here, span:]
            if conj:
                re, im = ar * br + ai * bi, ar * bi - ai * br
            else:
                re, im = ar * br - ai * bi, ar * bi + ai * br
            prod = jnp.concatenate([re, im], axis=1).astype(BF16)
            back = dot(prod, inner_inv[...])
            tc, ts = twist_cos[...], twist_sin[...]
            for c in range(step):
                re = back[c * groups : (c + 1) * groups, :span]
                im = back[c * groups : (c + 1) * groups, span:]
                both = jnp.concatenate([re * tc + im * ts, im * tc - re * ts], axis=0)
                field = dot(outer_inv[...], both.astype(BF16)) * scale
                rows = pl.ds(n * step + c, groups, stride=chans)
                time_buf[0, rows, :] = field[:, : span // 2]
                time_buf[1, rows, :] = field[:, span // 2 :]
            return carry
        lax.fori_loop(0, chans // step, body, 0)

    def product(a_ref, b_ref):
        return (a_ref[...].astype(F32) * b_ref[...].astype(F32)).astype(BF16).astype(F32)

    first_core = core == 0

    width = f_ref.shape[1]
    taps = f_ref[...].astype(F32)
    taps = jnp.where(first_core, taps[:, : width // 2], taps[:, width // 2 :]).T
    f_send[...] = fold(taps.reshape(groups, chans // 2, span))
    start_all(f_send, f_recv, 0)
    x_send[...] = spread(product(k_ref, v_ref).T, groups)
    start_all(x_send, x_recv, 1)
    g_send[...] = spread(product(q_ref, g_ref).T, groups)
    start_all(g_send, g_recv, 2)

    all_of(f_send, f_recv, 0).wait()
    swap = one(f_recv, f_other, 3, sibling)
    swap.start()
    swap.wait()
    held, other = unfold(f_recv[...]), unfold(f_other[...])
    taps = jnp.concatenate(
        [jnp.where(first_core, held, other), jnp.where(first_core, other, held)], axis=1
    )
    fill(taps)
    forward(spec_h)

    all_of(x_send, x_recv, 1).wait()
    fill(x_recv[...].astype(F32))
    forward(spec_x)
    inverse(spec_x, spec_h, False)
    c_send[...] = filled().astype(BF16)
    start_all(c_send, c_recv, 4)

    all_of(g_send, g_recv, 2).wait()
    fill(g_recv[...].astype(F32))
    forward(spec_g)
    inverse(spec_x, spec_g, True)
    corr = filled()
    low, high = corr[:, : chans // 2], corr[:, chans // 2 :]
    r_mine[...] = fold(jnp.where(first_core, high, low))
    swap = one(r_mine, r_other, 5, sibling)
    swap.start()
    kept = jnp.where(first_core, low, high)
    swap.wait()
    r_send[...] = fold(kept + unfold(r_other[...]))
    start_all(r_send, r_recv, 6)

    inverse(spec_h, spec_g, True)
    b_send[...] = filled().astype(BF16)
    start_all(b_send, b_recv, 7)

    skip = skip_ref[...]
    all_of(c_send, c_recv, 4).wait()
    mixed = gather_rows(c_recv[...]).T + skip * product(k_ref, v_ref)
    out_ref[...] = (q_ref[...].astype(F32) * mixed).astype(BF16)
    dq_ref[...] = (g_ref[...].astype(F32) * mixed).astype(BF16)

    all_of(r_send, r_recv, 6).wait()
    part = r_recv[...].astype(F32)
    rows = groups * chans // 2
    low = part[:, : chans // 2].reshape(rows, span // 2)
    high = part[:, chans // 2 :].reshape(rows, span // 2)
    h_send[...] = jnp.where(upper == 0, high, low).astype(BF16)
    swap = one(h_send, h_recv, 8, across)
    swap.start()

    all_of(b_send, b_recv, 7).wait()
    turned = gather_rows(b_recv[...]).T + skip * product(q_ref, g_ref)
    dk_ref[...] = (turned * v_ref[...].astype(F32)).astype(BF16)
    dv_ref[...] = (turned * k_ref[...].astype(F32)).astype(BF16)

    swap.wait()
    total = (jnp.where(upper == 0, low, high) + h_recv[...].astype(F32)).T
    quarter = span // 4
    t_send[...] = jnp.where(first_core, total[quarter:], total[:quarter])
    swap = one(t_send, t_recv, 9, sibling)
    swap.start()
    held = jnp.where(first_core, total[:quarter], total[quarter:])
    swap.wait()
    other = t_recv[...]
    df_ref[:, : width // 2] = jnp.where(first_core, held, other)
    df_ref[:, width // 2 :] = jnp.where(first_core, other, held)


def shards(queries, keys, values, cotangent, filter_param, skip):
    span, width = queries.shape
    groups = lax.axis_size("context")
    chans = width // groups
    length = groups * span
    scale = 1.0 / (length * math.sqrt(length))
    tables = make_tables(groups, span)
    whole = pl.BlockSpec(memory_space=pltpu.VMEM)
    big = pltpu.VMEM((groups, chans, span), BF16)
    small = pltpu.VMEM((groups, chans, span // 2), BF16)
    wide = jax.ShapeDtypeStruct((span, width), BF16)
    return pl.pallas_call(
        functools.partial(kernel, groups, scale),
        out_shape=(wide, wide, wide, wide, jax.ShapeDtypeStruct((span // 4, width), F32)),
        in_specs=[whole] * 12,
        out_specs=(whole,) * 5,
        scratch_shapes=[big] * 8
        + [small] * 7
        + [pltpu.VMEM((groups * chans // 2, span // 2), BF16)] * 2
        + [pltpu.VMEM((span // 4, width // 2), F32)] * 2
        + [pltpu.VMEM((2, groups * chans, span // 2), F32)]
        + [pltpu.VMEM((groups * chans, 2 * span), F32)] * 3
        + [pltpu.SemaphoreType.DMA((10,))] * 2,
        compiler_params=pltpu.CompilerParams(
            has_side_effects=True, vmem_limit_bytes=56 * 1024 * 1024
        ),
    )(queries, keys, values, cotangent, filter_param, skip.reshape(1, width), *tables)


def solution(mesh):
    placed = (
        P("context", "tensor"),
        P("context", "tensor"),
        P("context", "tensor"),
        P("context", "tensor"),
        P("context", None),
        P("tensor"),
    )
    return jax.shard_map(
        shards,
        mesh=mesh,
        in_specs=placed,
        out_specs=(
            P("context", "tensor"),
            P("context", "tensor"),
            P("context", "tensor"),
            P("context", "tensor"),
            P(("context", "tensor"), None),
        ),
        check_vma=False,
    )
```

```python
import functools
import math

import jax
import jax.numpy as jnp
import ml_dtypes
import numpy as np
from jax import lax
from jax.experimental import pallas as pl
from jax.experimental.pallas import tpu as pltpu
from jax.sharding import PartitionSpec as P

MESH = pl.DeviceIdType.MESH
F32 = jnp.float32
BF16 = jnp.bfloat16


def make_tables(blocks, span):
    length = blocks * span
    row = np.arange(blocks, dtype=np.float64)
    col = np.arange(span, dtype=np.float64)
    outer = 2.0 * np.pi * np.outer(row + 0.25, row) / blocks
    twist = 2.0 * np.pi * np.outer(row + 0.25, col) / length
    inner = 2.0 * np.pi * (np.outer(col, col) % span) / span
    outer_fwd = np.concatenate([np.cos(outer), -np.sin(outer)], axis=0)
    outer_inv = np.concatenate([np.cos(outer).T, -np.sin(outer).T], axis=1)
    cos, sin = np.cos(inner), np.sin(inner)
    inner_fwd = np.block([[cos, -sin], [sin, cos]])
    inner_inv = np.block([[cos, sin], [-sin, cos]])
    half = ml_dtypes.bfloat16
    return (
        outer_fwd.astype(half),
        outer_inv.astype(half),
        np.cos(twist).astype(np.float32),
        (-np.sin(twist)).astype(np.float32),
        inner_fwd.astype(half),
        inner_inv.astype(half),
    )


def dot(a, b):
    return jnp.dot(a, b, preferred_element_type=F32)


def spread(turned, groups):
    rows, span = turned.shape
    part = rows // (2 * groups)
    first = turned[: rows // 2].reshape(groups, part, span)
    second = turned[rows // 2 :].reshape(groups, part, span)
    return jnp.concatenate([first, second], axis=1).astype(BF16)


def gather_rows(blocks):
    groups, rows, span = blocks.shape
    wide = blocks.astype(F32)
    first = wide[:, : rows // 2].reshape(groups * rows // 2, span)
    second = wide[:, rows // 2 :].reshape(groups * rows // 2, span)
    return jnp.concatenate([first, second], axis=0)


def fold(rows):
    half = rows.shape[2] // 2
    return jnp.concatenate([rows[:, :, :half], rows[:, :, half:]], axis=1).astype(BF16)


def unfold(rows):
    part = rows.shape[1] // 2
    wide = rows.astype(F32)
    return jnp.concatenate([wide[:, :part], wide[:, part:]], axis=2)


def kernel(
    groups,
    side,
    scale,
    q_hbm, k_hbm, v_hbm, g_hbm, f_hbm,
    outer_fwd_hbm, outer_inv_hbm, twist_cos_hbm, twist_sin_hbm, inner_fwd_hbm, inner_inv_hbm,
    conv_ref, back_ref, df_ref,
    q_ref, k_ref, v_ref, g_ref, f_ref,
    outer_fwd, outer_inv, twist_cos, twist_sin, inner_fwd, inner_inv,
    x_send, x_recv, g_send, g_recv, c_send, c_recv, b_send, b_recv,
    f_send, f_recv, f_other, r_mine, r_other,
    r_send, r_mid, s_send, s_recv, t_send, t_recv,
    time_buf, spec_x, spec_h, spec_g,
    load_sem, send_sem, recv_sem, ring_sem, line_sem,
):
    span, width = q_ref.shape
    chans = x_send.shape[1]
    part = chans // 2
    ring = 2 * side
    step = min(4, chans)
    me = lax.axis_index("context")
    mine = lax.axis_index("tensor")
    core = mine % 2
    upper = mine // 2
    sibling = mine + 1 - 2 * core
    mx, mz, my = me // (side * side), (me // side) % side, me % side
    plane = upper * side + mz
    place = mx * side + my
    near = (mz // (side // 2) + upper) % 2
    first_core = core == 0

    def at_place(s):
        x, y = s // side, s % side
        return {"context": (x * side + mz) * side + y}

    def at_plane(p):
        return {"context": (mx * side + p % side) * side + my, "tensor": (p // side) * 2 + core}

    def along_x(s):
        return {"context": (((mx + s) % side) * side + mz) * side + my}

    def along_y(s):
        return {"context": (mx * side + mz) * side + (my + s) % side}

    def along_ring(s):
        return at_plane((plane + s) % ring)

    def greet(sem, where, count):
        def body(s, carry):
            pl.semaphore_signal(sem, inc=1, device_id=where(s), device_id_type=MESH)
            return carry
        lax.fori_loop(1, count, body, 0)

    def remote(src, dst, slot, where):
        return pltpu.make_async_remote_copy(
            src_ref=src, dst_ref=dst,
            send_sem=send_sem.at[slot], recv_sem=recv_sem.at[slot],
            device_id=where, device_id_type=MESH,
        )

    def start_all(src, dst, slot):
        def body(s, carry):
            to = (me + s) % groups
            remote(src.at[to], dst.at[me], slot, {"context": to}).start()
            return carry
        lax.fori_loop(1, groups, body, 0)
        dst[pl.ds(me, 1)] = src[pl.ds(me, 1)]

    def start_nearest(src, dst, slot):
        def body(s, carry):
            to = (me + s) % groups
            up = (near + ((to // side) % side) // (side // 2)) % 2
            remote(src.at[to], dst.at[me], slot, {"context": to, "tensor": 2 * up + core}).start()
            return carry
        lax.fori_loop(1, groups, body, 0)
        dst[pl.ds(me, 1)] = src[pl.ds(me, 1)]

    def start_plane(src, dst, slot):
        def body(s, carry):
            to = (place + s) % (side * side)
            remote(src.at[to // side, :, to % side], dst.at[place], slot, at_place(to)).start()
            return carry
        lax.fori_loop(1, side * side, body, 0)
        dst[pl.ds(place, 1)] = src[pl.ds(mx, 1), :, my]

    def start_ring(src, dst, slot):
        def body(s, carry):
            to = (plane + s) % ring
            remote(src.at[to], dst.at[plane], slot, at_plane(to)).start()
            return carry
        lax.fori_loop(1, ring, body, 0)
        dst[pl.ds(plane, 1)] = src[pl.ds(plane, 1)]

    def wait_all(dst, slot):
        blocks = dst.at[pl.ds(0, dst.shape[0] - 1)]
        remote(blocks, blocks, slot, {"tensor": sibling}).wait()

    def fill(field):
        flat = field.reshape(groups * chans, span)
        time_buf[0] = flat[:, : span // 2]
        time_buf[1] = flat[:, span // 2 :]

    def filled():
        flat = jnp.concatenate([time_buf[0], time_buf[1]], axis=1)
        return flat.reshape(groups, chans, span)

    def forward(dst):
        def body(n, carry):
            parts = []
            for c in range(step):
                rows = pl.ds(n * step + c, groups, stride=chans)
                field = jnp.concatenate([time_buf[0, rows, :], time_buf[1, rows, :]], axis=1)
                first = dot(outer_fwd[...], field.astype(BF16))
                re, im = first[:groups], first[groups:]
                tc, ts = twist_cos[...], twist_sin[...]
                parts.append(
                    jnp.concatenate([re * tc - im * ts, re * ts + im * tc], axis=1).astype(BF16)
                )
            rows = jnp.concatenate(parts, axis=0)
            here = pl.ds(pl.multiple_of(n * step * groups, step * groups), step * groups)
            dst[here, :] = dot(rows, inner_fwd[...])
            return carry
        lax.fori_loop(0, chans // step, body, 0)

    def inverse(a_ref, b_ref, conj):
        def body(n, carry):
            here = pl.ds(pl.multiple_of(n * step * groups, step * groups), step * groups)
            ar, ai = a_ref[here, :span], a_ref[here, span:]
            br, bi = b_ref[here, :span], b_ref[here, span:]
            if conj:
                re, im = ar * br + ai * bi, ar * bi - ai * br
            else:
                re, im = ar * br - ai * bi, ar * bi + ai * br
            prod = jnp.concatenate([re, im], axis=1).astype(BF16)
            back = dot(prod, inner_inv[...])
            tc, ts = twist_cos[...], twist_sin[...]
            for c in range(step):
                re = back[c * groups : (c + 1) * groups, :span]
                im = back[c * groups : (c + 1) * groups, span:]
                both = jnp.concatenate([re * tc + im * ts, im * tc - re * ts], axis=0)
                field = dot(outer_inv[...], both.astype(BF16)) * scale
                rows = pl.ds(n * step + c, groups, stride=chans)
                time_buf[0, rows, :] = field[:, : span // 2]
                time_buf[1, rows, :] = field[:, span // 2 :]
            return carry
        lax.fori_loop(0, chans // step, body, 0)

    def product(a_ref, b_ref):
        return (a_ref[...].astype(F32) * b_ref[...].astype(F32)).astype(BF16).astype(F32)

    loads = [
        pltpu.make_async_copy(src, dst, load_sem.at[n])
        for n, (src, dst) in enumerate(
            [
                (k_hbm, k_ref), (v_hbm, v_ref), (f_hbm, f_ref), (q_hbm, q_ref), (g_hbm, g_ref),
                (outer_fwd_hbm, outer_fwd), (twist_cos_hbm, twist_cos), (twist_sin_hbm, twist_sin),
                (inner_fwd_hbm, inner_fwd), (inner_inv_hbm, inner_inv), (outer_inv_hbm, outer_inv),
            ]
        )
    ]
    for load in loads:
        load.start()

    barrier = pltpu.get_barrier_semaphore()
    greet(barrier, along_x, side)
    greet(barrier, along_y, side)
    greet(barrier, along_ring, ring)
    pl.semaphore_signal(barrier, inc=1, device_id={"tensor": sibling}, device_id_type=MESH)
    loads[0].wait()
    loads[1].wait()
    x_send[...] = spread(product(k_ref, v_ref).T, groups)
    pl.semaphore_wait(barrier, 2 * side + ring - 2)
    greet(ring_sem, along_ring, ring)
    loads[2].wait()
    taps = f_ref[...].astype(F32)
    taps = jnp.where(first_core, taps[:, : width // 2], taps[:, width // 2 :]).T
    f_send[...] = fold(taps.reshape(groups, part, span))
    pl.semaphore_wait(ring_sem, ring - 1)
    greet(line_sem, along_x, side)
    pl.semaphore_wait(line_sem, side - 1)

    start_all(x_send, x_recv, 0)
    start_nearest(f_send, f_recv, 1)
    loads[3].wait()
    loads[4].wait()
    g_send[...] = spread(product(q_ref, g_ref).T, groups)
    start_all(g_send, g_recv, 2)
    for load in loads[5:]:
        load.wait()

    wait_all(f_recv, 1)
    swap = remote(f_recv, f_other, 3, {"tensor": sibling})
    swap.start()
    swap.wait()
    held, other = unfold(f_recv[...]), unfold(f_other[...])
    fill(
        jnp.concatenate(
            [jnp.where(first_core, held, other), jnp.where(first_core, other, held)], axis=1
        )
    )
    forward(spec_h)

    wait_all(x_recv, 0)
    fill(x_recv[...].astype(F32))
    forward(spec_x)
    inverse(spec_x, spec_h, False)
    c_send[...] = filled().astype(BF16)
    start_all(c_send, c_recv, 4)

    wait_all(g_recv, 2)
    fill(g_recv[...].astype(F32))
    forward(spec_g)
    inverse(spec_x, spec_g, True)
    corr = filled()
    low, high = corr[:, :part], corr[:, part:]
    r_mine[...] = fold(jnp.where(first_core, high, low))
    swap = remote(r_mine, r_other, 5, {"tensor": sibling})
    swap.start()
    kept = jnp.where(first_core, low, high)
    swap.wait()
    r_send[...] = fold(kept + unfold(r_other[...])).reshape(r_send.shape)
    start_plane(r_send, r_mid, 6)

    inverse(spec_h, spec_g, True)
    b_send[...] = filled().astype(BF16)

    wait_all(r_mid, 6)
    for z in range(side):
        rows = r_mid[:, z].astype(F32)
        s_send[z] = rows[:, :part].reshape(side * side * part, span // 2).astype(BF16)
        s_send[side + z] = rows[:, part:].reshape(side * side * part, span // 2).astype(BF16)
    start_ring(s_send, s_recv, 7)
    start_all(b_send, b_recv, 8)

    wait_all(c_recv, 4)
    conv_ref[...] = gather_rows(c_recv[...]).T.astype(BF16)

    wait_all(s_recv, 7)
    some = [s_recv[z].astype(F32) + s_recv[side + z].astype(F32) for z in range(side)]
    run = side * part
    total = jnp.concatenate(
        [some[z][x * run : (x + 1) * run] for x in range(side) for z in range(side)], axis=0
    ).T
    quarter = span // 4
    t_send[...] = jnp.where(first_core, total[quarter:], total[:quarter])
    swap = remote(t_send, t_recv, 9, {"tensor": sibling})
    swap.start()
    held = jnp.where(first_core, total[:quarter], total[quarter:])
    swap.wait()
    other = t_recv[...]
    df_ref[:, : width // 2] = jnp.where(first_core, held, other)
    df_ref[:, width // 2 :] = jnp.where(first_core, other, held)

    wait_all(b_recv, 8)
    back_ref[...] = gather_rows(b_recv[...]).T.astype(BF16)


def shards(queries, keys, values, cotangent, filter_param, skip):
    span, width = queries.shape
    groups = lax.axis_size("context")
    side = round(groups ** (1 / 3))
    chans = width // groups
    part = chans // 2
    length = groups * span
    scale = 1.0 / (length * math.sqrt(length))
    tables = make_tables(groups, span)
    whole = pl.BlockSpec(memory_space=pltpu.VMEM)
    anywhere = pl.BlockSpec(memory_space=pl.ANY)
    wide = pltpu.VMEM((span, width), BF16)
    big = pltpu.VMEM((groups, chans, span), BF16)
    small = pltpu.VMEM((groups, chans, span // 2), BF16)
    ring = pltpu.VMEM((2 * side, side * side * part, span // 2), BF16)
    conv, back, filter_grad = pl.pallas_call(
        functools.partial(kernel, groups, side, scale),
        out_shape=(
            jax.ShapeDtypeStruct((span, width), BF16),
            jax.ShapeDtypeStruct((span, width), BF16),
            jax.ShapeDtypeStruct((span // 4, width), F32),
        ),
        in_specs=[anywhere] * 11,
        out_specs=(whole,) * 3,
        scratch_shapes=[wide] * 5
        + [pltpu.VMEM(t.shape, t.dtype) for t in tables]
        + [big] * 8
        + [small] * 5
        + [
            pltpu.VMEM((side, side, side, chans, span // 2), BF16),
            pltpu.VMEM((side * side, side, chans, span // 2), BF16),
            ring,
            ring,
        ]
        + [pltpu.VMEM((span // 4, width // 2), F32)] * 2
        + [pltpu.VMEM((2, groups * chans, span // 2), F32)]
        + [pltpu.VMEM((groups * chans, 2 * span), F32)] * 3
        + [pltpu.SemaphoreType.DMA((11,))]
        + [pltpu.SemaphoreType.DMA((10,))] * 2
        + [pltpu.SemaphoreType.REGULAR] * 2,
        compiler_params=pltpu.CompilerParams(
            collective_id=0, has_side_effects=True, vmem_limit_bytes=56 * 1024 * 1024
        ),
    )(queries, keys, values, cotangent, filter_param, *tables)
    wide_q, wide_k = queries.astype(F32), keys.astype(F32)
    wide_v, wide_g = values.astype(F32), cotangent.astype(F32)
    gated = (wide_k * wide_v).astype(BF16).astype(F32)
    grad_in = (wide_q * wide_g).astype(BF16).astype(F32)
    mixed = conv.astype(F32) + skip * gated
    d_gated = back.astype(F32) + skip * grad_in
    return (
        (wide_q * mixed).astype(BF16),
        (wide_g * mixed).astype(BF16),
        (d_gated * wide_v).astype(BF16),
        (d_gated * wide_k).astype(BF16),
        filter_grad,
    )


def solution(mesh):
    placed = (
        P("context", "tensor"),
        P("context", "tensor"),
        P("context", "tensor"),
        P("context", "tensor"),
        P("context", None),
        P("tensor"),
    )
    return jax.shard_map(
        shards,
        mesh=mesh,
        in_specs=placed,
        out_specs=(
            P("context", "tensor"),
            P("context", "tensor"),
            P("context", "tensor"),
            P("context", "tensor"),
            P(("context", "tensor"), None),
        ),
        check_vma=False,
    )
```

```python
import functools
import math

import jax
import jax.numpy as jnp
import ml_dtypes
import numpy as np
from jax import lax
from jax.experimental import pallas as pl
from jax.experimental.pallas import tpu as pltpu
from jax.sharding import PartitionSpec as P

MESH = pl.DeviceIdType.MESH
F32 = jnp.float32
BF16 = jnp.bfloat16


def make_tables(blocks, span):
    length = blocks * span
    row = np.arange(blocks, dtype=np.float64)
    col = np.arange(span, dtype=np.float64)
    outer = 2.0 * np.pi * np.outer(row + 0.25, row) / blocks
    twist = 2.0 * np.pi * np.outer(row + 0.25, col) / length
    inner = 2.0 * np.pi * (np.outer(col, col) % span) / span
    outer_fwd = np.concatenate([np.cos(outer), -np.sin(outer)], axis=0)
    outer_inv = np.concatenate([np.cos(outer).T, -np.sin(outer).T], axis=1)
    cos, sin = np.cos(inner), np.sin(inner)
    inner_fwd = np.block([[cos, -sin], [sin, cos]])
    inner_inv = np.block([[cos, sin], [-sin, cos]])
    half = ml_dtypes.bfloat16
    return (
        outer_fwd.astype(half),
        outer_inv.astype(half),
        np.cos(twist).astype(np.float32),
        (-np.sin(twist)).astype(np.float32),
        inner_fwd.astype(half),
        inner_inv.astype(half),
    )


def dot(a, b):
    return jnp.dot(a, b, preferred_element_type=F32)


def spread(turned, groups):
    rows, span = turned.shape
    part = rows // (2 * groups)
    first = turned[: rows // 2].reshape(groups, part, span)
    second = turned[rows // 2 :].reshape(groups, part, span)
    return jnp.concatenate([first, second], axis=1).astype(BF16)


def gather_rows(blocks):
    groups, rows, span = blocks.shape
    wide = blocks.astype(F32)
    first = wide[:, : rows // 2].reshape(groups * rows // 2, span)
    second = wide[:, rows // 2 :].reshape(groups * rows // 2, span)
    return jnp.concatenate([first, second], axis=0)


def fold(rows):
    half = rows.shape[2] // 2
    return jnp.concatenate([rows[:, :, :half], rows[:, :, half:]], axis=1).astype(BF16)


def unfold(rows):
    part = rows.shape[1] // 2
    wide = rows.astype(F32)
    return jnp.concatenate([wide[:, :part], wide[:, part:]], axis=2)


def kernel(
    groups,
    side,
    scale,
    q_hbm, k_hbm, v_hbm, g_hbm, f_hbm, skip_ref,
    outer_fwd_hbm, outer_inv_hbm, twist_cos_hbm, twist_sin_hbm, inner_fwd_hbm, inner_inv_hbm,
    mixed_ref, turned_ref, df_ref,
    q_ref, k_ref, v_ref, g_ref, f_ref,
    outer_fwd, outer_inv, twist_cos, twist_sin, inner_fwd, inner_inv,
    x_send, x_recv, g_send, g_recv, c_send, c_recv, b_send, b_recv,
    f_send, f_recv, f_other, r_mine, r_other,
    r_send, r_mid, s_send, s_recv, t_send, t_recv,
    time_buf, kept_buf, spec_x, spec_h, spec_g,
    load_sem, send_sem, recv_sem, ring_sem,
):
    span, width = q_ref.shape
    chans = x_send.shape[1]
    part = chans // 2
    ring = 2 * side
    step = min(4, chans)
    me = lax.axis_index("context")
    mine = lax.axis_index("tensor")
    core = mine % 2
    upper = mine // 2
    sibling = mine + 1 - 2 * core
    mx, mz, my = me // (side * side), (me // side) % side, me % side
    plane = upper * side + mz
    place = mx * side + my
    near = (mz // (side // 2) + upper) % 2
    first_core = core == 0

    def at_place(s):
        x, y = s // side, s % side
        return {"context": (x * side + mz) * side + y}

    def at_plane(p):
        return {"context": (mx * side + p % side) * side + my, "tensor": (p // side) * 2 + core}

    def greet(sem, where, first, count):
        def body(s, carry):
            pl.semaphore_signal(sem, inc=1, device_id=where(s), device_id_type=MESH)
            return carry
        lax.fori_loop(first, count, body, 0)

    def remote(src, dst, slot, where):
        return pltpu.make_async_remote_copy(
            src_ref=src, dst_ref=dst,
            send_sem=send_sem.at[slot], recv_sem=recv_sem.at[slot],
            device_id=where, device_id_type=MESH,
        )

    def start_some(src, dst, slot, first, last):
        def body(s, carry):
            to = (me + s) % groups
            remote(src.at[to], dst.at[me], slot, {"context": to}).start()
            return carry
        lax.fori_loop(first, last, body, 0)

    def start_all(src, dst, slot):
        start_some(src, dst, slot, 1, groups)
        dst[pl.ds(me, 1)] = src[pl.ds(me, 1)]

    def start_nearest(src, dst, slot):
        def body(s, carry):
            to = (me + s) % groups
            up = (near + ((to // side) % side) // (side // 2)) % 2
            remote(src.at[to], dst.at[me], slot, {"context": to, "tensor": 2 * up + core}).start()
            return carry
        lax.fori_loop(1, groups, body, 0)
        dst[pl.ds(me, 1)] = src[pl.ds(me, 1)]

    def start_plane(src, dst, slot):
        def body(s, carry):
            to = (place + s) % (side * side)
            remote(src.at[to // side, :, to % side], dst.at[place], slot, at_place(to)).start()
            return carry
        lax.fori_loop(1, side * side, body, 0)
        dst[pl.ds(place, 1)] = src[pl.ds(mx, 1), :, my]

    def start_ring(src, dst, slot):
        def body(s, carry):
            to = (plane + s) % ring
            remote(src.at[to], dst.at[plane], slot, at_plane(to)).start()
            return carry
        lax.fori_loop(1, ring, body, 0)
        dst[pl.ds(plane, 1)] = src[pl.ds(plane, 1)]

    def wait_all(dst, slot):
        blocks = dst.at[pl.ds(0, dst.shape[0] - 1)]
        remote(blocks, blocks, slot, {"tensor": sibling}).wait()

    def fill(field):
        flat = field.reshape(groups * chans, span)
        time_buf[0] = flat[:, : span // 2]
        time_buf[1] = flat[:, span // 2 :]

    def filled():
        flat = jnp.concatenate([time_buf[0], time_buf[1]], axis=1)
        return flat.reshape(groups, chans, span)

    def forward(dst):
        def body(n, carry):
            parts = []
            for c in range(step):
                rows = pl.ds(n * step + c, groups, stride=chans)
                field = jnp.concatenate([time_buf[0, rows, :], time_buf[1, rows, :]], axis=1)
                first = dot(outer_fwd[...], field.astype(BF16))
                re, im = first[:groups], first[groups:]
                tc, ts = twist_cos[...], twist_sin[...]
                parts.append(
                    jnp.concatenate([re * tc - im * ts, re * ts + im * tc], axis=1).astype(BF16)
                )
            rows = jnp.concatenate(parts, axis=0)
            here = pl.ds(pl.multiple_of(n * step * groups, step * groups), step * groups)
            dst[here, :] = dot(rows, inner_fwd[...])
            return carry
        lax.fori_loop(0, chans // step, body, 0)

    def inverse(a_ref, b_ref, conj):
        def body(n, carry):
            here = pl.ds(pl.multiple_of(n * step * groups, step * groups), step * groups)
            ar, ai = a_ref[here, :span], a_ref[here, span:]
            br, bi = b_ref[here, :span], b_ref[here, span:]
            if conj:
                re, im = ar * br + ai * bi, ar * bi - ai * br
            else:
                re, im = ar * br - ai * bi, ar * bi + ai * br
            prod = jnp.concatenate([re, im], axis=1).astype(BF16)
            back = dot(prod, inner_inv[...])
            tc, ts = twist_cos[...], twist_sin[...]
            for c in range(step):
                re = back[c * groups : (c + 1) * groups, :span]
                im = back[c * groups : (c + 1) * groups, span:]
                both = jnp.concatenate([re * tc + im * ts, im * tc - re * ts], axis=0)
                field = dot(outer_inv[...], both.astype(BF16)) * scale
                rows = pl.ds(n * step + c, groups, stride=chans)
                time_buf[0, rows, :] = field[:, : span // 2]
                time_buf[1, rows, :] = field[:, span // 2 :]
            return carry
        lax.fori_loop(0, chans // step, body, 0)

    def product(a_ref, b_ref):
        return (a_ref[...].astype(F32) * b_ref[...].astype(F32)).astype(BF16).astype(F32)

    loads = [
        pltpu.make_async_copy(src, dst, load_sem.at[n])
        for n, (src, dst) in enumerate(
            [
                (k_hbm, k_ref), (v_hbm, v_ref), (f_hbm, f_ref), (q_hbm, q_ref), (g_hbm, g_ref),
                (outer_fwd_hbm, outer_fwd), (twist_cos_hbm, twist_cos), (twist_sin_hbm, twist_sin),
                (inner_fwd_hbm, inner_fwd), (inner_inv_hbm, inner_inv), (outer_inv_hbm, outer_inv),
            ]
        )
    ]
    for load in loads:
        load.start()

    barrier = pltpu.get_barrier_semaphore()
    greet(barrier, lambda s: {"context": (me + s) % groups}, 1, groups)
    greet(barrier, lambda s: at_plane((1 - upper) * side + s), 0, side)
    pl.semaphore_signal(barrier, inc=1, device_id={"tensor": sibling}, device_id_type=MESH)
    loads[0].wait()
    loads[1].wait()
    x_send[...] = spread(product(k_ref, v_ref).T, groups)
    loads[2].wait()
    taps = f_ref[...].astype(F32)
    taps = jnp.where(first_core, taps[:, : width // 2], taps[:, width // 2 :]).T
    f_send[...] = fold(taps.reshape(groups, part, span))
    pl.semaphore_wait(barrier, groups + side)
    greet(ring_sem, lambda s: at_plane((1 - upper) * side + s), 0, side)
    start_some(x_send, x_recv, 0, 1, groups // 2)
    x_recv[pl.ds(me, 1)] = x_send[pl.ds(me, 1)]
    loads[3].wait()
    loads[4].wait()
    g_send[...] = spread(product(q_ref, g_ref).T, groups)
    for load in loads[5:]:
        load.wait()
    pl.semaphore_wait(ring_sem, side)
    start_nearest(f_send, f_recv, 1)
    start_some(x_send, x_recv, 0, groups // 2, groups)
    start_all(g_send, g_recv, 2)

    wait_all(f_recv, 1)
    swap = remote(f_recv, f_other, 3, {"tensor": sibling})
    swap.start()
    swap.wait()
    held, other = unfold(f_recv[...]), unfold(f_other[...])
    fill(
        jnp.concatenate(
            [jnp.where(first_core, held, other), jnp.where(first_core, other, held)], axis=1
        )
    )
    forward(spec_h)

    wait_all(x_recv, 0)
    fill(x_recv[...].astype(F32))
    forward(spec_x)
    inverse(spec_x, spec_h, False)
    c_send[...] = filled().astype(BF16)

    start_all(c_send, c_recv, 4)
    wait_all(g_recv, 2)
    fill(g_recv[...].astype(F32))
    forward(spec_g)
    inverse(spec_x, spec_g, True)
    corr = filled()
    low, high = corr[:, :part], corr[:, part:]
    r_mine[...] = fold(jnp.where(first_core, high, low))
    swap = remote(r_mine, r_other, 5, {"tensor": sibling})
    swap.start()
    kept_buf[...] = jnp.where(first_core, low, high)

    inverse(spec_h, spec_g, True)
    b_send[...] = filled().astype(BF16)

    swap.wait()
    r_send[...] = fold(kept_buf[...] + unfold(r_other[...])).reshape(r_send.shape)
    start_plane(r_send, r_mid, 6)
    start_all(b_send, b_recv, 8)

    wait_all(r_mid, 6)
    for z in range(side):
        rows = r_mid[:, z].astype(F32)
        s_send[z] = rows[:, :part].reshape(side * side * part, span // 2).astype(BF16)
        s_send[side + z] = rows[:, part:].reshape(side * side * part, span // 2).astype(BF16)
    start_ring(s_send, s_recv, 7)

    wait_all(c_recv, 4)
    mixed_ref[...] = gather_rows(c_recv[...]).T + skip_ref[...] * product(k_ref, v_ref)

    wait_all(s_recv, 7)
    some = [s_recv[z].astype(F32) + s_recv[side + z].astype(F32) for z in range(side)]
    run = side * part
    total = jnp.concatenate(
        [some[z][x * run : (x + 1) * run] for x in range(side) for z in range(side)], axis=0
    ).T
    quarter = span // 4
    t_send[...] = jnp.where(first_core, total[quarter:], total[:quarter])
    swap = remote(t_send, t_recv, 9, {"tensor": sibling})
    swap.start()
    held = jnp.where(first_core, total[:quarter], total[quarter:])
    swap.wait()
    other = t_recv[...]
    df_ref[:, : width // 2] = jnp.where(first_core, held, other)
    df_ref[:, width // 2 :] = jnp.where(first_core, other, held)

    wait_all(b_recv, 8)
    turned_ref[...] = gather_rows(b_recv[...]).T + skip_ref[...] * product(q_ref, g_ref)


def shards(queries, keys, values, cotangent, filter_param, skip):
    span, width = queries.shape
    groups = lax.axis_size("context")
    side = round(groups ** (1 / 3))
    chans = width // groups
    part = chans // 2
    length = groups * span
    scale = 1.0 / (length * math.sqrt(length))
    tables = make_tables(groups, span)
    whole = pl.BlockSpec(memory_space=pltpu.VMEM)
    anywhere = pl.BlockSpec(memory_space=pl.ANY)
    wide = pltpu.VMEM((span, width), BF16)
    big = pltpu.VMEM((groups, chans, span), BF16)
    small = pltpu.VMEM((groups, chans, span // 2), BF16)
    ring = pltpu.VMEM((2 * side, side * side * part, span // 2), BF16)
    mixed, turned, filter_grad = pl.pallas_call(
        functools.partial(kernel, groups, side, scale),
        out_shape=(
            jax.ShapeDtypeStruct((span, width), F32),
            jax.ShapeDtypeStruct((span, width), F32),
            jax.ShapeDtypeStruct((span // 4, width), F32),
        ),
        in_specs=[anywhere] * 5 + [whole] + [anywhere] * 6,
        out_specs=(whole,) * 3,
        scratch_shapes=[wide] * 5
        + [pltpu.VMEM(t.shape, t.dtype) for t in tables]
        + [big] * 8
        + [small] * 5
        + [
            pltpu.VMEM((side, side, side, chans, span // 2), BF16),
            pltpu.VMEM((side * side, side, chans, span // 2), BF16),
            ring,
            ring,
        ]
        + [pltpu.VMEM((span // 4, width // 2), F32)] * 2
        + [pltpu.VMEM((2, groups * chans, span // 2), F32)]
        + [pltpu.VMEM((groups, part, span), F32)]
        + [pltpu.VMEM((groups * chans, 2 * span), F32)] * 3
        + [pltpu.SemaphoreType.DMA((11,))]
        + [pltpu.SemaphoreType.DMA((10,))] * 2
        + [pltpu.SemaphoreType.REGULAR],
        compiler_params=pltpu.CompilerParams(
            collective_id=0, has_side_effects=True, vmem_limit_bytes=56 * 1024 * 1024
        ),
    )(queries, keys, values, cotangent, filter_param, skip.reshape(1, width), *tables)
    return (
        (queries.astype(F32) * mixed).astype(BF16),
        (cotangent.astype(F32) * mixed).astype(BF16),
        (turned * values.astype(F32)).astype(BF16),
        (turned * keys.astype(F32)).astype(BF16),
        filter_grad,
    )


def solution(mesh):
    placed = (
        P("context", "tensor"),
        P("context", "tensor"),
        P("context", "tensor"),
        P("context", "tensor"),
        P("context", None),
        P("tensor"),
    )
    return jax.shard_map(
        shards,
        mesh=mesh,
        in_specs=placed,
        out_specs=(
            P("context", "tensor"),
            P("context", "tensor"),
            P("context", "tensor"),
            P("context", "tensor"),
            P(("context", "tensor"), None),
        ),
        check_vma=False,
    )
```

```python
import functools
import math

import jax
import jax.numpy as jnp
import ml_dtypes
import numpy as np
from jax import lax
from jax.experimental import pallas as pl
from jax.experimental.pallas import tpu as pltpu
from jax.sharding import PartitionSpec as P

MESH = pl.DeviceIdType.MESH
F32 = jnp.float32
BF16 = jnp.bfloat16


def make_tables(blocks, span):
    length = blocks * span
    row = np.arange(blocks, dtype=np.float64)
    col = np.arange(span, dtype=np.float64)
    outer = 2.0 * np.pi * np.outer(row + 0.25, row) / blocks
    twist = 2.0 * np.pi * np.outer(row + 0.25, col) / length
    inner = 2.0 * np.pi * (np.outer(col, col) % span) / span
    outer_fwd = np.concatenate([np.cos(outer), -np.sin(outer)], axis=0)
    outer_inv = np.concatenate([np.cos(outer).T, -np.sin(outer).T], axis=1)
    cos, sin = np.cos(inner), np.sin(inner)
    inner_fwd = np.block([[cos, -sin], [sin, cos]])
    inner_inv = np.block([[cos, sin], [-sin, cos]])
    half = ml_dtypes.bfloat16
    return (
        outer_fwd.astype(half),
        outer_inv.astype(half),
        np.cos(twist).astype(np.float32),
        (-np.sin(twist)).astype(np.float32),
        inner_fwd.astype(half),
        inner_inv.astype(half),
    )


def dot(a, b):
    return jnp.dot(a, b, preferred_element_type=F32)


def spread(turned, groups):
    rows, span = turned.shape
    part = rows // (2 * groups)
    first = turned[: rows // 2].reshape(groups, part, span)
    second = turned[rows // 2 :].reshape(groups, part, span)
    return jnp.concatenate([first, second], axis=1).astype(BF16)


def fold(rows):
    half = rows.shape[2] // 2
    return jnp.concatenate([rows[:, :, :half], rows[:, :, half:]], axis=1).astype(BF16)


def unfold(rows):
    part = rows.shape[1] // 2
    wide = rows.astype(F32)
    return jnp.concatenate([wide[:, :part], wide[:, part:]], axis=2)


def kernel(
    groups,
    side,
    scale,
    q_hbm, k_hbm, v_hbm, g_hbm, f_hbm, skip_ref,
    outer_fwd_hbm, outer_inv_hbm, twist_cos_hbm, twist_sin_hbm, inner_fwd_hbm, inner_inv_hbm,
    out_hbm, dq_hbm, dk_hbm, dv_hbm, df_hbm,
    q_ref, k_ref, v_ref, g_ref, f_ref,
    outer_fwd, outer_inv, twist_cos, twist_sin, inner_fwd, inner_inv,
    x_send, x_recv, g_send, g_recv, c_send, c_recv, b_send, b_recv,
    f_send, f_recv, f_other, r_mine, r_other,
    r_send, r_mid, s_send, s_recv, t_send, t_recv,
    time_buf, kept_buf, spec_x, spec_h, spec_g,
    out_ref, dq_ref, dk_ref, dv_ref, df_ref,
    save_sem, load_sem, send_sem, recv_sem, ring_sem,
):
    span, width = q_ref.shape
    chans = x_send.shape[1]
    part = chans // 2
    ring = 2 * side
    step = min(4, chans)
    me = lax.axis_index("context")
    mine = lax.axis_index("tensor")
    core = mine % 2
    upper = mine // 2
    sibling = mine + 1 - 2 * core
    mx, mz, my = me // (side * side), (me // side) % side, me % side
    plane = upper * side + mz
    place = mx * side + my
    near = (mz // (side // 2) + upper) % 2
    first_core = core == 0

    def at_place(s):
        x, y = s // side, s % side
        return {"context": (x * side + mz) * side + y}

    def at_plane(p):
        return {"context": (mx * side + p % side) * side + my, "tensor": (p // side) * 2 + core}

    def greet(sem, where, first, count):
        def body(s, carry):
            pl.semaphore_signal(sem, inc=1, device_id=where(s), device_id_type=MESH)
            return carry
        lax.fori_loop(first, count, body, 0)

    def remote(src, dst, slot, where):
        return pltpu.make_async_remote_copy(
            src_ref=src, dst_ref=dst,
            send_sem=send_sem.at[slot], recv_sem=recv_sem.at[slot],
            device_id=where, device_id_type=MESH,
        )

    def start_some(src, dst, slot, first, last):
        def body(s, carry):
            to = (me + s) % groups
            remote(src.at[to], dst.at[me], slot, {"context": to}).start()
            return carry
        lax.fori_loop(first, last, body, 0)

    def start_all(src, dst, slot):
        start_some(src, dst, slot, 1, groups)
        dst[pl.ds(me, 1)] = src[pl.ds(me, 1)]

    def start_nearest(src, dst, slot):
        def body(s, carry):
            to = (me + s) % groups
            up = (near + ((to // side) % side) // (side // 2)) % 2
            remote(src.at[to], dst.at[me], slot, {"context": to, "tensor": 2 * up + core}).start()
            return carry
        lax.fori_loop(1, groups, body, 0)
        dst[pl.ds(me, 1)] = src[pl.ds(me, 1)]

    def start_plane(src, dst, slot):
        def body(s, carry):
            to = (place + s) % (side * side)
            remote(src.at[to // side, :, to % side], dst.at[place], slot, at_place(to)).start()
            return carry
        lax.fori_loop(1, side * side, body, 0)
        dst[pl.ds(place, 1)] = src[pl.ds(mx, 1), :, my]

    def start_ring(src, dst, slot):
        def body(s, carry):
            to = (plane + s) % ring
            remote(src.at[to], dst.at[plane], slot, at_plane(to)).start()
            return carry
        lax.fori_loop(1, ring, body, 0)
        dst[pl.ds(plane, 1)] = src[pl.ds(plane, 1)]

    def wait_all(dst, slot):
        blocks = dst.at[pl.ds(0, dst.shape[0] - 1)]
        remote(blocks, blocks, slot, {"tensor": sibling}).wait()

    def fill(field):
        flat = field.reshape(groups * chans, span)
        time_buf[0] = flat[:, : span // 2]
        time_buf[1] = flat[:, span // 2 :]

    def filled():
        flat = jnp.concatenate([time_buf[0], time_buf[1]], axis=1)
        return flat.reshape(groups, chans, span)

    def forward(dst):
        def body(n, carry):
            parts = []
            for c in range(step):
                rows = pl.ds(n * step + c, groups, stride=chans)
                field = jnp.concatenate([time_buf[0, rows, :], time_buf[1, rows, :]], axis=1)
                first = dot(outer_fwd[...], field.astype(BF16))
                re, im = first[:groups], first[groups:]
                tc, ts = twist_cos[...], twist_sin[...]
                parts.append(
                    jnp.concatenate([re * tc - im * ts, re * ts + im * tc], axis=1).astype(BF16)
                )
            rows = jnp.concatenate(parts, axis=0)
            here = pl.ds(pl.multiple_of(n * step * groups, step * groups), step * groups)
            dst[here, :] = dot(rows, inner_fwd[...])
            return carry
        lax.fori_loop(0, chans // step, body, 0)

    def inverse(a_ref, b_ref, conj):
        def body(n, carry):
            here = pl.ds(pl.multiple_of(n * step * groups, step * groups), step * groups)
            ar, ai = a_ref[here, :span], a_ref[here, span:]
            br, bi = b_ref[here, :span], b_ref[here, span:]
            if conj:
                re, im = ar * br + ai * bi, ar * bi - ai * br
            else:
                re, im = ar * br - ai * bi, ar * bi + ai * br
            prod = jnp.concatenate([re, im], axis=1).astype(BF16)
            back = dot(prod, inner_inv[...])
            tc, ts = twist_cos[...], twist_sin[...]
            for c in range(step):
                re = back[c * groups : (c + 1) * groups, :span]
                im = back[c * groups : (c + 1) * groups, span:]
                both = jnp.concatenate([re * tc + im * ts, im * tc - re * ts], axis=0)
                field = dot(outer_inv[...], both.astype(BF16)) * scale
                rows = pl.ds(n * step + c, groups, stride=chans)
                time_buf[0, rows, :] = field[:, : span // 2]
                time_buf[1, rows, :] = field[:, span // 2 :]
            return carry
        lax.fori_loop(0, chans // step, body, 0)

    def product(a_ref, b_ref):
        return (a_ref[...].astype(F32) * b_ref[...].astype(F32)).astype(BF16).astype(F32)

    def save(src, dst, n):
        copy = pltpu.make_async_copy(src, dst, save_sem.at[n])
        copy.start()
        return copy

    def finish(recv, left, right, results, first):
        saves = []
        block = width // 4
        count = block // part
        for n in range(4):
            start = (n % 2) * count
            rows = recv[start : start + count].astype(F32)
            rows = rows[:, :part] if n < 2 else rows[:, part:]
            cols = slice(n * block, (n + 1) * block)
            direct = left[:, cols].astype(F32) * right[:, cols].astype(F32)
            direct = direct.astype(BF16).astype(F32)
            total = rows.reshape(block, span).T + skip_ref[:, cols] * direct
            for m, (factor, held, dst) in enumerate(results):
                held[:, cols] = (factor[:, cols].astype(F32) * total).astype(BF16)
                saves.append(save(held.at[:, cols], dst.at[:, cols], first + 2 * n + m))
        return saves

    loads = [
        pltpu.make_async_copy(src, dst, load_sem.at[n])
        for n, (src, dst) in enumerate(
            [
                (k_hbm, k_ref), (v_hbm, v_ref), (f_hbm, f_ref), (q_hbm, q_ref), (g_hbm, g_ref),
                (outer_fwd_hbm, outer_fwd), (twist_cos_hbm, twist_cos), (twist_sin_hbm, twist_sin),
                (inner_fwd_hbm, inner_fwd), (inner_inv_hbm, inner_inv), (outer_inv_hbm, outer_inv),
            ]
        )
    ]
    for load in loads:
        load.start()

    barrier = pltpu.get_barrier_semaphore()
    greet(barrier, lambda s: {"context": (me + s) % groups}, 1, groups)
    greet(barrier, lambda s: at_plane((1 - upper) * side + s), 0, side)
    pl.semaphore_signal(barrier, inc=1, device_id={"tensor": sibling}, device_id_type=MESH)
    loads[0].wait()
    loads[1].wait()
    x_send[...] = spread(product(k_ref, v_ref).T, groups)
    loads[2].wait()
    taps = f_ref[...].astype(F32)
    taps = jnp.where(first_core, taps[:, : width // 2], taps[:, width // 2 :]).T
    f_send[...] = fold(taps.reshape(groups, part, span))
    pl.semaphore_wait(barrier, groups + side)
    greet(ring_sem, lambda s: at_plane((1 - upper) * side + s), 0, side)
    start_some(x_send, x_recv, 0, 1, groups // 2)
    x_recv[pl.ds(me, 1)] = x_send[pl.ds(me, 1)]
    loads[3].wait()
    loads[4].wait()
    g_send[...] = spread(product(q_ref, g_ref).T, groups)
    for load in loads[5:]:
        load.wait()
    pl.semaphore_wait(ring_sem, side)
    start_nearest(f_send, f_recv, 1)
    start_some(x_send, x_recv, 0, groups // 2, groups)
    start_all(g_send, g_recv, 2)

    wait_all(f_recv, 1)
    swap = remote(f_recv, f_other, 3, {"tensor": sibling})
    swap.start()
    swap.wait()
    held, other = unfold(f_recv[...]), unfold(f_other[...])
    fill(
        jnp.concatenate(
            [jnp.where(first_core, held, other), jnp.where(first_core, other, held)], axis=1
        )
    )
    forward(spec_h)

    wait_all(x_recv, 0)
    fill(x_recv[...].astype(F32))
    forward(spec_x)
    inverse(spec_x, spec_h, False)
    c_send[...] = filled().astype(BF16)

    start_all(c_send, c_recv, 4)
    wait_all(g_recv, 2)
    fill(g_recv[...].astype(F32))
    forward(spec_g)
    inverse(spec_x, spec_g, True)
    corr = filled()
    low, high = corr[:, :part], corr[:, part:]
    r_mine[...] = fold(jnp.where(first_core, high, low))
    swap = remote(r_mine, r_other, 5, {"tensor": sibling})
    swap.start()
    kept_buf[...] = jnp.where(first_core, low, high)

    inverse(spec_h, spec_g, True)
    b_send[...] = filled().astype(BF16)

    swap.wait()
    r_send[...] = fold(kept_buf[...] + unfold(r_other[...])).reshape(r_send.shape)
    start_plane(r_send, r_mid, 6)
    start_all(b_send, b_recv, 8)

    wait_all(r_mid, 6)
    for z in range(side):
        rows = r_mid[:, z].astype(F32)
        s_send[z] = rows[:, :part].reshape(side * side * part, span // 2).astype(BF16)
        s_send[side + z] = rows[:, part:].reshape(side * side * part, span // 2).astype(BF16)
    start_ring(s_send, s_recv, 7)

    wait_all(c_recv, 4)
    saves = finish(
        c_recv, k_ref, v_ref, [(q_ref, out_ref, out_hbm), (g_ref, dq_ref, dq_hbm)], 0
    )

    wait_all(s_recv, 7)
    some = [s_recv[z].astype(F32) + s_recv[side + z].astype(F32) for z in range(side)]
    run = side * part
    total = jnp.concatenate(
        [some[z][x * run : (x + 1) * run] for x in range(side) for z in range(side)], axis=0
    ).T
    quarter = span // 4
    t_send[...] = jnp.where(first_core, total[quarter:], total[:quarter])
    swap = remote(t_send, t_recv, 9, {"tensor": sibling})
    swap.start()
    held = jnp.where(first_core, total[:quarter], total[quarter:])
    swap.wait()
    other = t_recv[...]
    df_ref[:, : width // 2] = jnp.where(first_core, held, other)
    df_ref[:, width // 2 :] = jnp.where(first_core, other, held)
    saves.append(save(df_ref, df_hbm, 16))

    wait_all(b_recv, 8)
    saves += finish(
        b_recv, q_ref, g_ref, [(v_ref, dk_ref, dk_hbm), (k_ref, dv_ref, dv_hbm)], 8
    )
    for copy in saves:
        copy.wait()


def hand_over(*refs):
    load_sem, save_sem = refs[15:]
    loads, saves = [], []
    for n in range(5):
        src, dst, held = refs[n], refs[5 + n], refs[10 + n]
        part = src.shape[0] // 2
        for m in range(2):
            rows = pl.ds(m * part, part)
            loads.append(pltpu.make_async_copy(src.at[rows], held.at[rows], load_sem.at[n, m]))
            saves.append(pltpu.make_async_copy(held.at[rows], dst.at[rows], save_sem.at[n, m]))
    for load in loads:
        load.start()
    for load, copy in zip(loads, saves):
        load.wait()
        copy.start()
    for copy in saves:
        copy.wait()


def shards(queries, keys, values, cotangent, filter_param, skip):
    span, width = queries.shape
    groups = lax.axis_size("context")
    side = round(groups ** (1 / 3))
    chans = width // groups
    part = chans // 2
    length = groups * span
    scale = 1.0 / (length * math.sqrt(length))
    tables = make_tables(groups, span)
    whole = pl.BlockSpec(memory_space=pltpu.VMEM)
    anywhere = pl.BlockSpec(memory_space=pl.ANY)
    wide = pltpu.VMEM((span, width), BF16)
    big = pltpu.VMEM((groups, chans, span), BF16)
    small = pltpu.VMEM((groups, chans, span // 2), BF16)
    ring = pltpu.VMEM((2 * side, side * side * part, span // 2), BF16)
    shape = jax.ShapeDtypeStruct((span, width), BF16)
    shapes = (shape,) * 4 + (jax.ShapeDtypeStruct((span // 4, width), F32),)
    results = pl.pallas_call(
        functools.partial(kernel, groups, side, scale),
        out_shape=shapes,
        in_specs=[anywhere] * 5 + [whole] + [anywhere] * 6,
        out_specs=(anywhere,) * 5,
        scratch_shapes=[wide] * 5
        + [pltpu.VMEM(t.shape, t.dtype) for t in tables]
        + [big] * 8
        + [small] * 5
        + [
            pltpu.VMEM((side, side, side, chans, span // 2), BF16),
            pltpu.VMEM((side * side, side, chans, span // 2), BF16),
            ring,
            ring,
        ]
        + [pltpu.VMEM((span // 4, width // 2), F32)] * 2
        + [pltpu.VMEM((2, groups * chans, span // 2), F32)]
        + [pltpu.VMEM((groups, part, span), F32)]
        + [pltpu.VMEM((groups * chans, 2 * span), F32)] * 3
        + [wide] * 4
        + [pltpu.VMEM((span // 4, width), F32)]
        + [pltpu.SemaphoreType.DMA((17,)), pltpu.SemaphoreType.DMA((11,))]
        + [pltpu.SemaphoreType.DMA((10,))] * 2
        + [pltpu.SemaphoreType.REGULAR],
        compiler_params=pltpu.CompilerParams(
            collective_id=0, has_side_effects=True, vmem_limit_bytes=56 * 1024 * 1024
        ),
    )(queries, keys, values, cotangent, filter_param, skip.reshape(1, width), *tables)
    return pl.pallas_call(
        hand_over,
        out_shape=shapes,
        in_specs=[anywhere] * 5,
        out_specs=(anywhere,) * 5,
        scratch_shapes=[pltpu.VMEM(r.shape, r.dtype) for r in shapes]
        + [pltpu.SemaphoreType.DMA((5, 2))] * 2,
    )(*results)


def solution(mesh):
    placed = (
        P("context", "tensor"),
        P("context", "tensor"),
        P("context", "tensor"),
        P("context", "tensor"),
        P("context", None),
        P("tensor"),
    )
    return jax.shard_map(
        shards,
        mesh=mesh,
        in_specs=placed,
        out_specs=(
            P("context", "tensor"),
            P("context", "tensor"),
            P("context", "tensor"),
            P("context", "tensor"),
            P(("context", "tensor"), None),
        ),
        check_vma=False,
    )
```

```python
import functools
import math

import jax
import jax.numpy as jnp
import ml_dtypes
import numpy as np
from jax import lax
from jax.experimental import pallas as pl
from jax.experimental.pallas import tpu as pltpu
from jax.sharding import PartitionSpec as P

MESH = pl.DeviceIdType.MESH
F32 = jnp.float32
BF16 = jnp.bfloat16


def make_tables(blocks, span):
    length = blocks * span
    row = np.arange(blocks, dtype=np.float64)
    col = np.arange(span, dtype=np.float64)
    outer = 2.0 * np.pi * np.outer(row + 0.25, row) / blocks
    twist = 2.0 * np.pi * np.outer(row + 0.25, col) / length
    inner = 2.0 * np.pi * (np.outer(col, col) % span) / span
    outer_fwd = np.concatenate([np.cos(outer), -np.sin(outer)], axis=0)
    outer_inv = np.concatenate([np.cos(outer).T, -np.sin(outer).T], axis=1)
    cos, sin = np.cos(inner), np.sin(inner)
    inner_fwd = np.block([[cos, -sin], [sin, cos]])
    inner_inv = np.block([[cos, sin], [-sin, cos]])
    half = ml_dtypes.bfloat16
    return (
        outer_fwd.astype(half),
        outer_inv.astype(half),
        np.cos(twist).astype(np.float32),
        (-np.sin(twist)).astype(np.float32),
        inner_fwd.astype(half),
        inner_inv.astype(half),
    )


def dot(a, b):
    return jnp.dot(a, b, preferred_element_type=F32)


def spread(turned, groups):
    rows, span = turned.shape
    part = rows // (2 * groups)
    first = turned[: rows // 2].reshape(groups, part, span)
    second = turned[rows // 2 :].reshape(groups, part, span)
    return jnp.concatenate([first, second], axis=1).astype(BF16)


def fold(rows):
    half = rows.shape[2] // 2
    return jnp.concatenate([rows[:, :, :half], rows[:, :, half:]], axis=1).astype(BF16)


def unfold(rows):
    part = rows.shape[1] // 2
    wide = rows.astype(F32)
    return jnp.concatenate([wide[:, :part], wide[:, part:]], axis=2)


def kernel(
    groups,
    side,
    scale,
    q_hbm, k_hbm, v_hbm, g_hbm, f_hbm, skip_ref,
    outer_fwd_hbm, outer_inv_hbm, twist_cos_hbm, twist_sin_hbm, inner_fwd_hbm, inner_inv_hbm,
    out_hbm, dq_hbm, dk_hbm, dv_hbm, df_hbm,
    q_ref, k_ref, v_ref, g_ref, f_ref,
    outer_fwd, outer_inv, twist_cos, twist_sin, inner_fwd, inner_inv,
    x_send, x_recv, g_send, g_recv,
    c0_send, c0_recv, c1_send, c1_recv, b0_send, b0_recv, b1_send, b1_recv,
    f_send, f_recv, f_other, r_mine, r_other,
    r_send, r_mid, s_send, s_recv, t_send, t_recv, own_buf,
    time_buf, kept_buf, spec_x, spec_h, spec_g,
    out_ref, dq_ref, dk_ref, dv_ref, df_ref,
    save_sem, load_sem, send_sem, recv_sem, ring_sem,
):
    span, width = q_ref.shape
    chans = x_send.shape[1]
    part = chans // 2
    ring = 2 * side
    step = min(4, chans)
    me = lax.axis_index("context")
    mine = lax.axis_index("tensor")
    core = mine % 2
    upper = mine // 2
    sibling = mine + 1 - 2 * core
    mx, mz, my = me // (side * side), (me // side) % side, me % side
    plane = upper * side + mz
    place = mx * side + my
    near = (mz // (side // 2) + upper) % 2
    first_core = core == 0

    def at_place(s):
        x, y = s // side, s % side
        return {"context": (x * side + mz) * side + y}

    def at_plane(p):
        return {"context": (mx * side + p % side) * side + my, "tensor": (p // side) * 2 + core}

    def greet(sem, where, first, count):
        def body(s, carry):
            pl.semaphore_signal(sem, inc=1, device_id=where(s), device_id_type=MESH)
            return carry
        lax.fori_loop(first, count, body, 0)

    def remote(src, dst, slot, where):
        return pltpu.make_async_remote_copy(
            src_ref=src, dst_ref=dst,
            send_sem=send_sem.at[slot], recv_sem=recv_sem.at[slot],
            device_id=where, device_id_type=MESH,
        )

    def start_some(src, dst, slot, first, last):
        def body(s, carry):
            to = (me + s) % groups
            remote(src.at[to], dst.at[me], slot, {"context": to}).start()
            return carry
        lax.fori_loop(first, last, body, 0)

    def start_all(src, dst, slot):
        start_some(src, dst, slot, 1, groups)
        dst[pl.ds(me, 1)] = src[pl.ds(me, 1)]

    def start_nearest(src, dst, slot):
        def body(s, carry):
            to = (me + s) % groups
            up = (near + ((to // side) % side) // (side // 2)) % 2
            remote(src.at[to], dst.at[me], slot, {"context": to, "tensor": 2 * up + core}).start()
            return carry
        lax.fori_loop(1, groups, body, 0)
        dst[pl.ds(me, 1)] = src[pl.ds(me, 1)]

    def start_plane(src, dst, slot):
        def body(s, carry):
            to = (place + s) % (side * side)
            remote(src.at[to // side, :, to % side], dst.at[place], slot, at_place(to)).start()
            return carry
        lax.fori_loop(1, side * side, body, 0)
        dst[pl.ds(place, 1)] = src[pl.ds(mx, 1), :, my]

    def start_ring(src, dst, slot):
        def body(s, carry):
            to = (plane + s) % ring
            remote(src.at[to], dst.at[plane], slot, at_plane(to)).start()
            return carry
        lax.fori_loop(1, ring, body, 0)
        dst[pl.ds(plane, 1)] = src[pl.ds(plane, 1)]

    def wait_all(dst, slot):
        blocks = dst.at[pl.ds(0, dst.shape[0] - 1)]
        remote(blocks, blocks, slot, {"tensor": sibling}).wait()

    def fill(field):
        flat = field.reshape(groups * chans, span)
        time_buf[0] = flat[:, : span // 2]
        time_buf[1] = flat[:, span // 2 :]

    def packed(n):
        low = time_buf[0].reshape(groups, chans, span // 2)[:, n * part : (n + 1) * part]
        high = time_buf[1].reshape(groups, chans, span // 2)[:, n * part : (n + 1) * part]
        return jnp.concatenate([low, high], axis=1)

    def forward(dst, first=0, last=chans // step):
        def body(n, carry):
            parts = []
            for c in range(step):
                rows = pl.ds(n * step + c, groups, stride=chans)
                field = jnp.concatenate([time_buf[0, rows, :], time_buf[1, rows, :]], axis=1)
                first = dot(outer_fwd[...], field.astype(BF16))
                re, im = first[:groups], first[groups:]
                tc, ts = twist_cos[...], twist_sin[...]
                parts.append(
                    jnp.concatenate([re * tc - im * ts, re * ts + im * tc], axis=1).astype(BF16)
                )
            rows = jnp.concatenate(parts, axis=0)
            here = pl.ds(pl.multiple_of(n * step * groups, step * groups), step * groups)
            dst[here, :] = dot(rows, inner_fwd[...])
            return carry
        lax.fori_loop(first, last, body, 0)

    def inverse(a_ref, b_ref, conj, first=0, last=chans // step):
        def body(n, carry):
            here = pl.ds(pl.multiple_of(n * step * groups, step * groups), step * groups)
            ar, ai = a_ref[here, :span], a_ref[here, span:]
            br, bi = b_ref[here, :span], b_ref[here, span:]
            if conj:
                re, im = ar * br + ai * bi, ar * bi - ai * br
            else:
                re, im = ar * br - ai * bi, ar * bi + ai * br
            prod = jnp.concatenate([re, im], axis=1).astype(BF16)
            back = dot(prod, inner_inv[...])
            tc, ts = twist_cos[...], twist_sin[...]
            for c in range(step):
                re = back[c * groups : (c + 1) * groups, :span]
                im = back[c * groups : (c + 1) * groups, span:]
                both = jnp.concatenate([re * tc + im * ts, im * tc - re * ts], axis=0)
                field = dot(outer_inv[...], both.astype(BF16)) * scale
                rows = pl.ds(n * step + c, groups, stride=chans)
                time_buf[0, rows, :] = field[:, : span // 2]
                time_buf[1, rows, :] = field[:, span // 2 :]
            return carry
        lax.fori_loop(first, last, body, 0)

    def product(a_ref, b_ref):
        return (a_ref[...].astype(F32) * b_ref[...].astype(F32)).astype(BF16).astype(F32)

    def save(src, dst, n):
        copy = pltpu.make_async_copy(src, dst, save_sem.at[n])
        copy.start()
        return copy

    def finish(half, recv, left, right, results, first):
        saves = []
        block = width // 4
        count = block // part
        for n in (2 * half, 2 * half + 1):
            start = (n % 2) * count
            rows = unfold(recv[start : start + count])
            cols = slice(n * block, (n + 1) * block)
            direct = left[:, cols].astype(F32) * right[:, cols].astype(F32)
            direct = direct.astype(BF16).astype(F32)
            total = rows.reshape(block, span).T + skip_ref[:, cols] * direct
            for m, (factor, held, dst) in enumerate(results):
                held[:, cols] = (factor[:, cols].astype(F32) * total).astype(BF16)
                saves.append(save(held.at[:, cols], dst.at[:, cols], first + 2 * n + m))
        return saves

    loads = [
        pltpu.make_async_copy(src, dst, load_sem.at[n])
        for n, (src, dst) in enumerate(
            [
                (k_hbm, k_ref), (v_hbm, v_ref), (f_hbm, f_ref), (q_hbm, q_ref), (g_hbm, g_ref),
                (outer_fwd_hbm, outer_fwd), (twist_cos_hbm, twist_cos), (twist_sin_hbm, twist_sin),
                (inner_fwd_hbm, inner_fwd), (inner_inv_hbm, inner_inv), (outer_inv_hbm, outer_inv),
            ]
        )
    ]
    for load in loads:
        load.start()

    barrier = pltpu.get_barrier_semaphore()
    greet(barrier, lambda s: {"context": (me + s) % groups}, 1, groups)
    greet(barrier, lambda s: at_plane((1 - upper) * side + s), 0, side)
    pl.semaphore_signal(barrier, inc=1, device_id={"tensor": sibling}, device_id_type=MESH)
    loads[0].wait()
    loads[1].wait()
    x_send[...] = spread(product(k_ref, v_ref).T, groups)
    loads[2].wait()
    taps = f_ref[...].astype(F32)
    taps = jnp.where(first_core, taps[:, : width // 2], taps[:, width // 2 :]).T
    f_send[...] = fold(taps.reshape(groups, part, span))
    pl.semaphore_wait(barrier, groups + side)
    greet(ring_sem, lambda s: at_plane((1 - upper) * side + s), 0, side)
    start_some(x_send, x_recv, 0, 1, groups // 2)
    x_recv[pl.ds(me, 1)] = x_send[pl.ds(me, 1)]
    loads[3].wait()
    loads[4].wait()
    g_send[...] = spread(product(q_ref, g_ref).T, groups)
    for load in loads[5:]:
        load.wait()
    pl.semaphore_wait(ring_sem, side)
    start_nearest(f_send, f_recv, 1)
    start_some(x_send, x_recv, 0, groups // 2, groups)
    start_all(g_send, g_recv, 2)

    wait_all(f_recv, 1)
    swap = remote(f_recv, f_other, 3, {"tensor": sibling})
    swap.start()
    swap.wait()
    held, other = unfold(f_recv[...]), unfold(f_other[...])
    fill(
        jnp.concatenate(
            [jnp.where(first_core, held, other), jnp.where(first_core, other, held)], axis=1
        )
    )
    forward(spec_h)

    wait_all(x_recv, 0)
    fill(x_recv[...].astype(F32))
    mid = chans // step // 2
    forward(spec_x, 0, mid)
    inverse(spec_x, spec_h, False, 0, mid)
    c0_send[...] = packed(0).astype(BF16)
    start_all(c0_send, c0_recv, 4)
    forward(spec_x, mid, 2 * mid)
    inverse(spec_x, spec_h, False, mid, 2 * mid)
    c1_send[...] = packed(1).astype(BF16)
    start_all(c1_send, c1_recv, 10)

    wait_all(g_recv, 2)
    fill(g_recv[...].astype(F32))
    forward(spec_g)
    inverse(spec_x, spec_g, True)
    low, high = packed(0), packed(1)
    r_mine[...] = jnp.where(first_core, high, low).astype(BF16)
    swap = remote(r_mine, r_other, 5, {"tensor": sibling})
    swap.start()
    kept_buf[...] = jnp.where(first_core, low, high)

    inverse(spec_h, spec_g, True, 0, mid)
    b0_send[...] = packed(0).astype(BF16)
    swap.wait()
    r_send[...] = (kept_buf[...] + r_other[...].astype(F32)).astype(BF16).reshape(r_send.shape)
    start_plane(r_send, r_mid, 6)
    start_all(b0_send, b0_recv, 8)
    inverse(spec_h, spec_g, True, mid, 2 * mid)
    b1_send[...] = packed(1).astype(BF16)
    start_all(b1_send, b1_recv, 11)

    wait_all(r_mid, 6)
    for z in range(side):
        rows = r_mid[:, z].astype(F32)
        s_send[z] = rows[:, :part].reshape(side * side * part, span // 2).astype(BF16)
        s_send[side + z] = rows[:, part:].reshape(side * side * part, span // 2).astype(BF16)
    start_ring(s_send, s_recv, 7)

    forth = [(q_ref, out_ref, out_hbm), (g_ref, dq_ref, dq_hbm)]
    back = [(v_ref, dk_ref, dk_hbm), (k_ref, dv_ref, dv_hbm)]
    wait_all(c0_recv, 4)
    saves = finish(0, c0_recv, k_ref, v_ref, forth, 0)
    wait_all(c1_recv, 10)
    saves += finish(1, c1_recv, k_ref, v_ref, forth, 0)
    wait_all(b0_recv, 8)
    saves += finish(0, b0_recv, q_ref, g_ref, back, 8)

    wait_all(s_recv, 7)
    some = [s_recv[z].astype(F32) + s_recv[side + z].astype(F32) for z in range(side)]
    run = side * part
    total = jnp.concatenate(
        [some[z][x * run : (x + 1) * run] for x in range(side) for z in range(side)], axis=0
    ).T
    quarter = span // 4
    t_send[...] = jnp.where(first_core, total[quarter:], total[:quarter])
    swap = remote(t_send, t_recv, 9, {"tensor": sibling})
    swap.start()
    own_buf[...] = jnp.where(first_core, total[:quarter], total[quarter:])
    wait_all(b1_recv, 11)
    saves += finish(1, b1_recv, q_ref, g_ref, back, 8)
    swap.wait()
    held, other = own_buf[...], t_recv[...]
    df_ref[:, : width // 2] = jnp.where(first_core, held, other)
    df_ref[:, width // 2 :] = jnp.where(first_core, other, held)
    saves.append(save(df_ref, df_hbm, 16))
    for copy in saves:
        copy.wait()


def hand_over(*refs):
    load_sem, save_sem = refs[15:]
    loads, saves = [], []
    for n in range(5):
        src, dst, held = refs[n], refs[5 + n], refs[10 + n]
        part = src.shape[0] // 2
        for m in range(2):
            rows = pl.ds(m * part, part)
            loads.append(pltpu.make_async_copy(src.at[rows], held.at[rows], load_sem.at[n, m]))
            saves.append(pltpu.make_async_copy(held.at[rows], dst.at[rows], save_sem.at[n, m]))
    for load in loads:
        load.start()
    for load, copy in zip(loads, saves):
        load.wait()
        copy.start()
    for copy in saves:
        copy.wait()


def shards(queries, keys, values, cotangent, filter_param, skip):
    span, width = queries.shape
    groups = lax.axis_size("context")
    side = round(groups ** (1 / 3))
    chans = width // groups
    part = chans // 2
    length = groups * span
    scale = 1.0 / (length * math.sqrt(length))
    tables = make_tables(groups, span)
    whole = pl.BlockSpec(memory_space=pltpu.VMEM)
    anywhere = pl.BlockSpec(memory_space=pl.ANY)
    wide = pltpu.VMEM((span, width), BF16)
    big = pltpu.VMEM((groups, chans, span), BF16)
    small = pltpu.VMEM((groups, chans, span // 2), BF16)
    ring = pltpu.VMEM((2 * side, side * side * part, span // 2), BF16)
    shape = jax.ShapeDtypeStruct((span, width), BF16)
    shapes = (shape,) * 4 + (jax.ShapeDtypeStruct((span // 4, width), F32),)
    results = pl.pallas_call(
        functools.partial(kernel, groups, side, scale),
        out_shape=shapes,
        in_specs=[anywhere] * 5 + [whole] + [anywhere] * 6,
        out_specs=(anywhere,) * 5,
        scratch_shapes=[wide] * 5
        + [pltpu.VMEM(t.shape, t.dtype) for t in tables]
        + [big] * 4
        + [small] * 13
        + [
            pltpu.VMEM((side, side, side, chans, span // 2), BF16),
            pltpu.VMEM((side * side, side, chans, span // 2), BF16),
            ring,
            ring,
        ]
        + [pltpu.VMEM((span // 4, width // 2), F32)] * 3
        + [pltpu.VMEM((2, groups * chans, span // 2), F32)]
        + [pltpu.VMEM((groups, chans, span // 2), F32)]
        + [pltpu.VMEM((groups * chans, 2 * span), F32)] * 3
        + [wide] * 4
        + [pltpu.VMEM((span // 4, width), F32)]
        + [pltpu.SemaphoreType.DMA((17,)), pltpu.SemaphoreType.DMA((11,))]
        + [pltpu.SemaphoreType.DMA((12,))] * 2
        + [pltpu.SemaphoreType.REGULAR],
        compiler_params=pltpu.CompilerParams(
            collective_id=0, has_side_effects=True, vmem_limit_bytes=56 * 1024 * 1024
        ),
    )(queries, keys, values, cotangent, filter_param, skip.reshape(1, width), *tables)
    return pl.pallas_call(
        hand_over,
        out_shape=shapes,
        in_specs=[anywhere] * 5,
        out_specs=(anywhere,) * 5,
        scratch_shapes=[pltpu.VMEM(r.shape, r.dtype) for r in shapes]
        + [pltpu.SemaphoreType.DMA((5, 2))] * 2,
    )(*results)


def solution(mesh):
    placed = (
        P("context", "tensor"),
        P("context", "tensor"),
        P("context", "tensor"),
        P("context", "tensor"),
        P("context", None),
        P("tensor"),
    )
    return jax.shard_map(
        shards,
        mesh=mesh,
        in_specs=placed,
        out_specs=(
            P("context", "tensor"),
            P("context", "tensor"),
            P("context", "tensor"),
            P("context", "tensor"),
            P(("context", "tensor"), None),
        ),
        check_vma=False,
    )
```

```python
import functools
import math

import jax
import jax.numpy as jnp
import ml_dtypes
import numpy as np
from jax import lax
from jax.experimental import pallas as pl
from jax.experimental.pallas import tpu as pltpu
from jax.sharding import PartitionSpec as P

MESH = pl.DeviceIdType.MESH
F32 = jnp.float32
BF16 = jnp.bfloat16


def make_tables(blocks, span):
    length = blocks * span
    row = np.arange(blocks, dtype=np.float64)
    col = np.arange(span, dtype=np.float64)
    outer = 2.0 * np.pi * np.outer(row + 0.25, row) / blocks
    twist = 2.0 * np.pi * np.outer(row + 0.25, col) / length
    inner = 2.0 * np.pi * (np.outer(col, col) % span) / span
    outer_fwd = np.concatenate([np.cos(outer), -np.sin(outer)], axis=0)
    outer_inv = np.concatenate([np.cos(outer).T, -np.sin(outer).T], axis=1)
    cos, sin = np.cos(inner), np.sin(inner)
    inner_fwd = np.block([[cos, -sin], [sin, cos]])
    inner_inv = np.block([[cos, sin], [-sin, cos]])
    half = ml_dtypes.bfloat16
    return (
        outer_fwd.astype(half),
        outer_inv.astype(half),
        np.cos(twist).astype(np.float32),
        (-np.sin(twist)).astype(np.float32),
        inner_fwd.astype(half),
        inner_inv.astype(half),
    )


def dot(a, b):
    return jnp.dot(a, b, preferred_element_type=F32)


def spread(turned, groups):
    rows, span = turned.shape
    part = rows // (2 * groups)
    first = turned[: rows // 2].reshape(groups, part, span)
    second = turned[rows // 2 :].reshape(groups, part, span)
    return jnp.concatenate([first, second], axis=1).astype(BF16)


def fold(rows):
    half = rows.shape[2] // 2
    return jnp.concatenate([rows[:, :, :half], rows[:, :, half:]], axis=1).astype(BF16)


def unfold(rows):
    part = rows.shape[1] // 2
    wide = rows.astype(F32)
    return jnp.concatenate([wide[:, :part], wide[:, part:]], axis=2)


def kernel(
    groups,
    side,
    scale,
    q_hbm, k_hbm, v_hbm, g_hbm, f_hbm, skip_ref,
    outer_fwd_hbm, outer_inv_hbm, twist_cos_hbm, twist_sin_hbm, inner_fwd_hbm, inner_inv_hbm,
    out_hbm, dq_hbm, dk_hbm, dv_hbm, df_hbm,
    q_ref, k_ref, v_ref, g_ref, f_ref,
    outer_fwd, outer_inv, twist_cos, twist_sin, inner_fwd, inner_inv,
    x_send, x_recv, g_send, g_recv,
    c0_send, c0_recv, c1_send, c1_recv, b0_send, b0_recv, b1_send, b1_recv,
    f_send, f_recv, f_other, r_mine, r_other,
    e_send, e_recv, e_kept, r_send, r_mid, s_send, s_recv, t_send, t_recv, own_buf,
    time_buf, kept_buf, spec_x, spec_h, spec_g,
    out_ref, dq_ref, dk_ref, dv_ref, df_ref,
    save_sem, load_sem, send_sem, recv_sem, ring_sem,
):
    span, width = q_ref.shape
    chans = x_send.shape[1]
    part = chans // 2
    step = min(4, chans)
    me = lax.axis_index("context")
    mine = lax.axis_index("tensor")
    core = mine % 2
    upper = mine // 2
    sibling = mine + 1 - 2 * core
    mx, mz, my = me // (side * side), (me // side) % side, me % side
    place = mx * side + my
    near = (mz // (side // 2) + upper) % 2
    first_core = core == 0
    first_half = upper == 0

    def level_of(z, up):
        return (z + up * (side // 2)) % side

    def group_of(to, up):
        x, z, y = to // (side * side), (to // side) % side, to % side
        return (x * side + level_of(z, up)) * side + y

    own = group_of(me, upper)

    def at_place(s):
        x, y = s // side, s % side
        return {"context": (x * side + mz) * side + y}

    def at_plane(p):
        return {"context": (mx * side + p % side) * side + my, "tensor": (p // side) * 2 + core}

    def greet(sem, where, first, count):
        def body(s, carry):
            pl.semaphore_signal(sem, inc=1, device_id=where(s), device_id_type=MESH)
            return carry
        lax.fori_loop(first, count, body, 0)

    def remote(src, dst, slot, where):
        return pltpu.make_async_remote_copy(
            src_ref=src, dst_ref=dst,
            send_sem=send_sem.at[slot], recv_sem=recv_sem.at[slot],
            device_id=where, device_id_type=MESH,
        )

    def start_some(src, dst, slot, first, last):
        def body(s, carry):
            to = (me + s) % groups
            remote(src.at[group_of(to, upper)], dst.at[me], slot, {"context": to}).start()
            return carry
        lax.fori_loop(first, last, body, 0)

    def start_out(src, dst, slot):
        start_some(src, dst, slot, 1, groups)
        dst[pl.ds(me, 1)] = src[pl.ds(own, 1)]

    def start_home(src, dst, slot):
        def body(s, carry):
            to = (me + s) % groups
            remote(src.at[to], dst.at[own], slot, {"context": to}).start()
            return carry
        lax.fori_loop(1, groups, body, 0)
        dst[pl.ds(own, 1)] = src[pl.ds(me, 1)]

    def start_nearest(src, dst, slot):
        def body(s, carry):
            to = (me + s) % groups
            up = (near + ((to // side) % side) // (side // 2)) % 2
            where = {"context": to, "tensor": 2 * up + core}
            remote(src.at[group_of(to, up)], dst.at[me], slot, where).start()
            return carry
        lax.fori_loop(1, groups, body, 0)
        dst[pl.ds(me, 1)] = src[pl.ds(own, 1)]

    def start_plane(src, dst, slot):
        def body(s, carry):
            to = (place + s) % (side * side)
            remote(src.at[to], dst.at[place], slot, at_place(to)).start()
            return carry
        lax.fori_loop(1, side * side, body, 0)
        dst[pl.ds(place, 1)] = src[pl.ds(place, 1)]

    def start_line(src, dst, slot):
        def body(s, carry):
            to = (mz + s) % side
            remote(src.at[to], dst.at[level_of(mz, upper)], slot, at_plane(upper * side + to)).start()
            return carry
        lax.fori_loop(1, side, body, 0)
        dst[pl.ds(level_of(mz, upper), 1)] = src[pl.ds(mz, 1)]

    def wait_all(dst, slot):
        blocks = dst.at[pl.ds(0, dst.shape[0] - 1)]
        remote(blocks, blocks, slot, {"tensor": sibling}).wait()

    def fill(field):
        flat = field.reshape(groups * chans, span)
        time_buf[0] = flat[:, : span // 2]
        time_buf[1] = flat[:, span // 2 :]

    def packed(n):
        low = time_buf[0].reshape(groups, chans, span // 2)[:, n * part : (n + 1) * part]
        high = time_buf[1].reshape(groups, chans, span // 2)[:, n * part : (n + 1) * part]
        return jnp.concatenate([low, high], axis=1)

    def forward(dst, first=0, last=chans // step):
        def body(n, carry):
            parts = []
            for c in range(step):
                rows = pl.ds(n * step + c, groups, stride=chans)
                field = jnp.concatenate([time_buf[0, rows, :], time_buf[1, rows, :]], axis=1)
                first = dot(outer_fwd[...], field.astype(BF16))
                re, im = first[:groups], first[groups:]
                tc, ts = twist_cos[...], twist_sin[...]
                parts.append(
                    jnp.concatenate([re * tc - im * ts, re * ts + im * tc], axis=1).astype(BF16)
                )
            rows = jnp.concatenate(parts, axis=0)
            here = pl.ds(pl.multiple_of(n * step * groups, step * groups), step * groups)
            dst[here, :] = dot(rows, inner_fwd[...])
            return carry
        lax.fori_loop(first, last, body, 0)

    def inverse(a_ref, b_ref, conj, first=0, last=chans // step):
        def body(n, carry):
            here = pl.ds(pl.multiple_of(n * step * groups, step * groups), step * groups)
            ar, ai = a_ref[here, :span], a_ref[here, span:]
            br, bi = b_ref[here, :span], b_ref[here, span:]
            if conj:
                re, im = ar * br + ai * bi, ar * bi - ai * br
            else:
                re, im = ar * br - ai * bi, ar * bi + ai * br
            prod = jnp.concatenate([re, im], axis=1).astype(BF16)
            back = dot(prod, inner_inv[...])
            tc, ts = twist_cos[...], twist_sin[...]
            for c in range(step):
                re = back[c * groups : (c + 1) * groups, :span]
                im = back[c * groups : (c + 1) * groups, span:]
                both = jnp.concatenate([re * tc + im * ts, im * tc - re * ts], axis=0)
                field = dot(outer_inv[...], both.astype(BF16)) * scale
                rows = pl.ds(n * step + c, groups, stride=chans)
                time_buf[0, rows, :] = field[:, : span // 2]
                time_buf[1, rows, :] = field[:, span // 2 :]
            return carry
        lax.fori_loop(first, last, body, 0)

    def product(a_ref, b_ref):
        return (a_ref[...].astype(F32) * b_ref[...].astype(F32)).astype(BF16).astype(F32)

    def save(src, dst, n):
        copy = pltpu.make_async_copy(src, dst, save_sem.at[n])
        copy.start()
        return copy

    def finish(half, recv, left, right, results, first):
        saves = []
        block = width // 4
        count = block // part
        for n in (2 * half, 2 * half + 1):
            start = (n % 2) * count
            rows = unfold(recv[start : start + count])
            cols = slice(n * block, (n + 1) * block)
            direct = left[:, cols].astype(F32) * right[:, cols].astype(F32)
            direct = direct.astype(BF16).astype(F32)
            total = rows.reshape(block, span).T + skip_ref[:, cols] * direct
            for m, (factor, held, dst) in enumerate(results):
                held[:, cols] = (factor[:, cols].astype(F32) * total).astype(BF16)
                saves.append(save(held.at[:, cols], dst.at[:, cols], first + 2 * n + m))
        return saves

    loads = [
        pltpu.make_async_copy(src, dst, load_sem.at[n])
        for n, (src, dst) in enumerate(
            [
                (k_hbm, k_ref), (v_hbm, v_ref), (f_hbm, f_ref), (q_hbm, q_ref), (g_hbm, g_ref),
                (outer_fwd_hbm, outer_fwd), (twist_cos_hbm, twist_cos), (twist_sin_hbm, twist_sin),
                (inner_fwd_hbm, inner_fwd), (inner_inv_hbm, inner_inv), (outer_inv_hbm, outer_inv),
            ]
        )
    ]
    for load in loads:
        load.start()

    barrier = pltpu.get_barrier_semaphore()
    greet(barrier, lambda s: {"context": (me + s) % groups}, 1, groups)
    greet(barrier, lambda s: at_plane((1 - upper) * side + s), 0, side)
    pl.semaphore_signal(barrier, inc=1, device_id={"tensor": sibling}, device_id_type=MESH)
    loads[0].wait()
    loads[1].wait()
    x_send[...] = spread(product(k_ref, v_ref).T, groups)
    loads[2].wait()
    taps = f_ref[...].astype(F32)
    taps = jnp.where(first_core, taps[:, : width // 2], taps[:, width // 2 :]).T
    f_send[...] = fold(taps.reshape(groups, part, span))
    pl.semaphore_wait(barrier, groups + side)
    greet(ring_sem, lambda s: at_plane((1 - upper) * side + s), 0, side)
    start_some(x_send, x_recv, 0, 1, groups // 2)
    x_recv[pl.ds(me, 1)] = x_send[pl.ds(own, 1)]
    loads[3].wait()
    loads[4].wait()
    g_send[...] = spread(product(q_ref, g_ref).T, groups)
    for load in loads[5:]:
        load.wait()
    pl.semaphore_wait(ring_sem, side)
    start_nearest(f_send, f_recv, 1)
    start_some(x_send, x_recv, 0, groups // 2, groups)
    start_out(g_send, g_recv, 2)

    wait_all(f_recv, 1)
    swap = remote(f_recv, f_other, 3, {"tensor": sibling})
    swap.start()
    swap.wait()
    held, other = unfold(f_recv[...]), unfold(f_other[...])
    fill(
        jnp.concatenate(
            [jnp.where(first_core, held, other), jnp.where(first_core, other, held)], axis=1
        )
    )
    forward(spec_h)

    wait_all(x_recv, 0)
    fill(x_recv[...].astype(F32))
    mid = chans // step // 2
    forward(spec_x, 0, mid)
    inverse(spec_x, spec_h, False, 0, mid)
    c0_send[...] = packed(0).astype(BF16)
    start_home(c0_send, c0_recv, 4)
    forward(spec_x, mid, 2 * mid)
    inverse(spec_x, spec_h, False, mid, 2 * mid)
    c1_send[...] = packed(1).astype(BF16)
    start_home(c1_send, c1_recv, 10)

    wait_all(g_recv, 2)
    fill(g_recv[...].astype(F32))
    forward(spec_g)
    inverse(spec_x, spec_g, True)
    low, high = packed(0), packed(1)
    r_mine[...] = jnp.where(first_core, high, low).astype(BF16)
    swap = remote(r_mine, r_other, 5, {"tensor": sibling})
    swap.start()
    kept_buf[...] = jnp.where(first_core, low, high)

    inverse(spec_h, spec_g, True, 0, mid)
    b0_send[...] = packed(0).astype(BF16)
    swap.wait()
    total = kept_buf[...] + r_other[...].astype(F32)
    low, high = total[:, :part], total[:, part:]
    e_send[...] = jnp.where(first_half, high, low).reshape(e_send.shape).astype(BF16)
    partner = at_plane((1 - upper) * side + (mz + side // 2) % side)
    trade = remote(e_send, e_recv, 12, partner)
    trade.start()
    e_kept[...] = jnp.where(first_half, low, high).reshape(e_kept.shape)
    start_home(b0_send, b0_recv, 8)
    inverse(spec_h, spec_g, True, mid, 2 * mid)
    b1_send[...] = packed(1).astype(BF16)
    start_home(b1_send, b1_recv, 11)

    trade.wait()
    total = (e_kept[...] + e_recv[...].astype(F32)).reshape(side, side, side, part, span // 2)
    for x in range(side):
        for y in range(side):
            r_send[x * side + y] = jnp.concatenate(
                [total[x, z, y] for z in range(side)], axis=0
            ).astype(BF16)
    start_plane(r_send, r_mid, 6)

    forth = [(q_ref, out_ref, out_hbm), (g_ref, dq_ref, dq_hbm)]
    back = [(v_ref, dk_ref, dk_hbm), (k_ref, dv_ref, dv_hbm)]
    wait_all(c0_recv, 4)
    saves = finish(0, c0_recv, k_ref, v_ref, forth, 0)
    wait_all(r_mid, 6)
    rows = r_mid[...].astype(F32)
    for z in range(side):
        level = rows[:, z * part : (z + 1) * part]
        s_send[z] = level.reshape(side * side * part, span // 2).astype(BF16)
    start_line(s_send, s_recv, 7)
    wait_all(c1_recv, 10)
    saves += finish(1, c1_recv, k_ref, v_ref, forth, 0)
    wait_all(b0_recv, 8)
    saves += finish(0, b0_recv, q_ref, g_ref, back, 8)

    wait_all(s_recv, 7)
    some = [s_recv[z].astype(F32) for z in range(side)]
    run = side * part
    total = jnp.concatenate(
        [some[z][x * run : (x + 1) * run] for x in range(side) for z in range(side)], axis=0
    ).T
    quarter = span // 4
    t_send[...] = jnp.where(first_core, total[quarter:], total[:quarter])
    swap = remote(t_send, t_recv, 9, {"tensor": sibling})
    swap.start()
    own_buf[...] = jnp.where(first_core, total[:quarter], total[quarter:])
    wait_all(b1_recv, 11)
    saves += finish(1, b1_recv, q_ref, g_ref, back, 8)
    swap.wait()
    held, other = own_buf[...], t_recv[...]
    df_ref[:, : width // 2] = jnp.where(first_core, held, other)
    df_ref[:, width // 2 :] = jnp.where(first_core, other, held)
    saves.append(save(df_ref, df_hbm, 16))
    for copy in saves:
        copy.wait()


def hand_over(*refs):
    load_sem, save_sem = refs[15:]
    loads, saves = [], []
    for n in range(5):
        src, dst, held = refs[n], refs[5 + n], refs[10 + n]
        part = src.shape[0] // 2
        for m in range(2):
            rows = pl.ds(m * part, part)
            loads.append(pltpu.make_async_copy(src.at[rows], held.at[rows], load_sem.at[n, m]))
            saves.append(pltpu.make_async_copy(held.at[rows], dst.at[rows], save_sem.at[n, m]))
    for load in loads:
        load.start()
    for load, copy in zip(loads, saves):
        load.wait()
        copy.start()
    for copy in saves:
        copy.wait()


def shards(queries, keys, values, cotangent, filter_param, skip):
    span, width = queries.shape
    groups = lax.axis_size("context")
    side = round(groups ** (1 / 3))
    chans = width // groups
    part = chans // 2
    length = groups * span
    scale = 1.0 / (length * math.sqrt(length))
    tables = make_tables(groups, span)
    whole = pl.BlockSpec(memory_space=pltpu.VMEM)
    anywhere = pl.BlockSpec(memory_space=pl.ANY)
    wide = pltpu.VMEM((span, width), BF16)
    big = pltpu.VMEM((groups, chans, span), BF16)
    small = pltpu.VMEM((groups, chans, span // 2), BF16)
    rows = pltpu.VMEM((groups * part, span // 2), BF16)
    line = pltpu.VMEM((side, side * side * part, span // 2), BF16)
    shape = jax.ShapeDtypeStruct((span, width), BF16)
    shapes = (shape,) * 4 + (jax.ShapeDtypeStruct((span // 4, width), F32),)
    results = pl.pallas_call(
        functools.partial(kernel, groups, side, scale),
        out_shape=shapes,
        in_specs=[anywhere] * 5 + [whole] + [anywhere] * 6,
        out_specs=(anywhere,) * 5,
        scratch_shapes=[wide] * 5
        + [pltpu.VMEM(t.shape, t.dtype) for t in tables]
        + [big] * 4
        + [small] * 13
        + [
            rows,
            rows,
            pltpu.VMEM((groups * part, span // 2), F32),
            pltpu.VMEM((side * side, side * part, span // 2), BF16),
            pltpu.VMEM((side * side, side * part, span // 2), BF16),
            line,
            line,
        ]
        + [pltpu.VMEM((span // 4, width // 2), F32)] * 3
        + [pltpu.VMEM((2, groups * chans, span // 2), F32)]
        + [pltpu.VMEM((groups, chans, span // 2), F32)]
        + [pltpu.VMEM((groups * chans, 2 * span), F32)] * 3
        + [wide] * 4
        + [pltpu.VMEM((span // 4, width), F32)]
        + [pltpu.SemaphoreType.DMA((17,)), pltpu.SemaphoreType.DMA((11,))]
        + [pltpu.SemaphoreType.DMA((13,))] * 2
        + [pltpu.SemaphoreType.REGULAR],
        compiler_params=pltpu.CompilerParams(
            collective_id=0, has_side_effects=True, vmem_limit_bytes=56 * 1024 * 1024
        ),
    )(queries, keys, values, cotangent, filter_param, skip.reshape(1, width), *tables)
    return pl.pallas_call(
        hand_over,
        out_shape=shapes,
        in_specs=[anywhere] * 5,
        out_specs=(anywhere,) * 5,
        scratch_shapes=[pltpu.VMEM(r.shape, r.dtype) for r in shapes]
        + [pltpu.SemaphoreType.DMA((5, 2))] * 2,
    )(*results)


def solution(mesh):
    placed = (
        P("context", "tensor"),
        P("context", "tensor"),
        P("context", "tensor"),
        P("context", "tensor"),
        P("context", None),
        P("tensor"),
    )
    return jax.shard_map(
        shards,
        mesh=mesh,
        in_specs=placed,
        out_specs=(
            P("context", "tensor"),
            P("context", "tensor"),
            P("context", "tensor"),
            P("context", "tensor"),
            P(("context", "tensor"), None),
        ),
        check_vma=False,
    )
```

```python
import functools
import math

import jax
import jax.numpy as jnp
import ml_dtypes
import numpy as np
from jax import lax
from jax.experimental import pallas as pl
from jax.experimental.pallas import tpu as pltpu
from jax.sharding import PartitionSpec as P

MESH = pl.DeviceIdType.MESH
F32 = jnp.float32
BF16 = jnp.bfloat16


def make_tables(blocks, span):
    length = blocks * span
    row = np.arange(blocks, dtype=np.float64)
    col = np.arange(span, dtype=np.float64)
    outer = 2.0 * np.pi * np.outer(row + 0.25, row) / blocks
    twist = 2.0 * np.pi * np.outer(row + 0.25, col) / length
    inner = 2.0 * np.pi * (np.outer(col, col) % span) / span
    outer_fwd = np.concatenate([np.cos(outer), -np.sin(outer)], axis=0)
    outer_inv = np.concatenate([np.cos(outer).T, -np.sin(outer).T], axis=1)
    cos, sin = np.cos(inner), np.sin(inner)
    inner_fwd = np.block([[cos, -sin], [sin, cos]])
    inner_inv = np.block([[cos, sin], [-sin, cos]])
    half = ml_dtypes.bfloat16
    return (
        outer_fwd.astype(half),
        outer_inv.astype(half),
        np.cos(twist).astype(np.float32),
        (-np.sin(twist)).astype(np.float32),
        inner_fwd.astype(half),
        inner_inv.astype(half),
    )


def dot(a, b):
    return jnp.dot(a, b, preferred_element_type=F32)


def spread(turned, groups):
    rows, span = turned.shape
    part = rows // (2 * groups)
    first = turned[: rows // 2].reshape(groups, part, span)
    second = turned[rows // 2 :].reshape(groups, part, span)
    return jnp.concatenate([first, second], axis=1).astype(BF16)


def fold(rows):
    half = rows.shape[2] // 2
    return jnp.concatenate([rows[:, :, :half], rows[:, :, half:]], axis=1).astype(BF16)


def unfold(rows):
    part = rows.shape[1] // 2
    wide = rows.astype(F32)
    return jnp.concatenate([wide[:, :part], wide[:, part:]], axis=2)


def kernel(
    groups,
    side,
    scale,
    q_hbm, k_hbm, v_hbm, g_hbm, f_hbm, skip_ref,
    outer_fwd_hbm, outer_inv_hbm, twist_cos_hbm, twist_sin_hbm, inner_fwd_hbm, inner_inv_hbm,
    out_hbm, dq_hbm, dk_hbm, dv_hbm, df_hbm,
    q_ref, k_ref, v_ref, g_ref, f_ref,
    outer_fwd, outer_inv, twist_cos, twist_sin, inner_fwd, inner_inv,
    x_send, x_recv, g_send, g_recv,
    c0_send, c0_recv, c1_send, c1_recv, b0_send, b0_recv, b1_send, b1_recv,
    f_send, f_recv, f_other, r_mine, r_other,
    e0_send, e1_send, e0_recv, e1_recv, e_kept, r0_send, r1_send, r0_mid, r1_mid, s_send, s_recv, t_send, t_recv, own_buf,
    time_buf, kept_buf, spec_x, spec_h, spec_g,
    out_ref, dq_ref, dk_ref, dv_ref, df_ref,
    save_sem, load_sem, send_sem, recv_sem, ring_sem,
):
    e_send, e_recv = (e0_send, e1_send), (e0_recv, e1_recv)
    r_send, r_mid = (r0_send, r1_send), (r0_mid, r1_mid)
    span, width = q_ref.shape
    chans = x_send.shape[1]
    part = chans // 2
    half = side // 2
    step = min(4, chans)
    me = lax.axis_index("context")
    mine = lax.axis_index("tensor")
    core = mine % 2
    upper = mine // 2
    sibling = mine + 1 - 2 * core
    mx, mz, my = me // (side * side), (me // side) % side, me % side
    place = mx * side + my
    near = (mz // (side // 2) + upper) % 2
    first_core = core == 0
    first_half = upper == 0

    def level_of(z, up):
        return (z + up * (side // 2)) % side

    def group_of(to, up):
        x, z, y = to // (side * side), (to // side) % side, to % side
        return (x * side + level_of(z, up)) * side + y

    own = group_of(me, upper)

    def at_place(s):
        x, y = s // side, s % side
        return {"context": (x * side + mz) * side + y}

    def at_plane(p):
        return {"context": (mx * side + p % side) * side + my, "tensor": (p // side) * 2 + core}

    def greet(sem, where, first, count):
        def body(s, carry):
            pl.semaphore_signal(sem, inc=1, device_id=where(s), device_id_type=MESH)
            return carry
        lax.fori_loop(first, count, body, 0)

    def remote(src, dst, slot, where):
        return pltpu.make_async_remote_copy(
            src_ref=src, dst_ref=dst,
            send_sem=send_sem.at[slot], recv_sem=recv_sem.at[slot],
            device_id=where, device_id_type=MESH,
        )

    def start_some(src, dst, slot, first, last):
        def body(s, carry):
            to = (me + s) % groups
            remote(src.at[group_of(to, upper)], dst.at[me], slot, {"context": to}).start()
            return carry
        lax.fori_loop(first, last, body, 0)

    def start_out(src, dst, slot):
        start_some(src, dst, slot, 1, groups)
        dst[pl.ds(me, 1)] = src[pl.ds(own, 1)]

    def start_home(src, dst, slot):
        def body(s, carry):
            to = (me + s) % groups
            remote(src.at[to], dst.at[own], slot, {"context": to}).start()
            return carry
        lax.fori_loop(1, groups, body, 0)
        dst[pl.ds(own, 1)] = src[pl.ds(me, 1)]

    def start_nearest(src, dst, slot):
        def body(s, carry):
            to = (me + s) % groups
            up = (near + ((to // side) % side) // (side // 2)) % 2
            where = {"context": to, "tensor": 2 * up + core}
            remote(src.at[group_of(to, up)], dst.at[me], slot, where).start()
            return carry
        lax.fori_loop(1, groups, body, 0)
        dst[pl.ds(me, 1)] = src[pl.ds(own, 1)]

    def start_plane(src, dst, slot):
        def body(s, carry):
            to = (place + s) % (side * side)
            remote(src.at[to], dst.at[place], slot, at_place(to)).start()
            return carry
        lax.fori_loop(1, side * side, body, 0)
        dst[pl.ds(place, 1)] = src[pl.ds(place, 1)]

    def start_line(src, dst, slot, first):
        def body(s, carry):
            to = first + s

            @pl.when(to != mz)
            def _():
                where = at_plane(upper * side + to)
                remote(src.at[to], dst.at[level_of(mz, upper)], slot, where).start()

            return carry
        lax.fori_loop(0, side // 2, body, 0)

    def wait_all(dst, slot):
        blocks = dst.at[pl.ds(0, dst.shape[0] - 1)]
        remote(blocks, blocks, slot, {"tensor": sibling}).wait()

    def fill(field):
        flat = field.reshape(groups * chans, span)
        time_buf[0] = flat[:, : span // 2]
        time_buf[1] = flat[:, span // 2 :]

    def packed(n):
        low = time_buf[0].reshape(groups, chans, span // 2)[:, n * part : (n + 1) * part]
        high = time_buf[1].reshape(groups, chans, span // 2)[:, n * part : (n + 1) * part]
        return jnp.concatenate([low, high], axis=1)

    def forward(dst, first=0, last=chans // step):
        def body(n, carry):
            parts = []
            for c in range(step):
                rows = pl.ds(n * step + c, groups, stride=chans)
                field = jnp.concatenate([time_buf[0, rows, :], time_buf[1, rows, :]], axis=1)
                first = dot(outer_fwd[...], field.astype(BF16))
                re, im = first[:groups], first[groups:]
                tc, ts = twist_cos[...], twist_sin[...]
                parts.append(
                    jnp.concatenate([re * tc - im * ts, re * ts + im * tc], axis=1).astype(BF16)
                )
            rows = jnp.concatenate(parts, axis=0)
            here = pl.ds(pl.multiple_of(n * step * groups, step * groups), step * groups)
            dst[here, :] = dot(rows, inner_fwd[...])
            return carry
        lax.fori_loop(first, last, body, 0)

    def inverse(a_ref, b_ref, conj, first=0, last=chans // step):
        def body(n, carry):
            here = pl.ds(pl.multiple_of(n * step * groups, step * groups), step * groups)
            ar, ai = a_ref[here, :span], a_ref[here, span:]
            br, bi = b_ref[here, :span], b_ref[here, span:]
            if conj:
                re, im = ar * br + ai * bi, ar * bi - ai * br
            else:
                re, im = ar * br - ai * bi, ar * bi + ai * br
            prod = jnp.concatenate([re, im], axis=1).astype(BF16)
            back = dot(prod, inner_inv[...])
            tc, ts = twist_cos[...], twist_sin[...]
            for c in range(step):
                re = back[c * groups : (c + 1) * groups, :span]
                im = back[c * groups : (c + 1) * groups, span:]
                both = jnp.concatenate([re * tc + im * ts, im * tc - re * ts], axis=0)
                field = dot(outer_inv[...], both.astype(BF16)) * scale
                rows = pl.ds(n * step + c, groups, stride=chans)
                time_buf[0, rows, :] = field[:, : span // 2]
                time_buf[1, rows, :] = field[:, span // 2 :]
            return carry
        lax.fori_loop(first, last, body, 0)

    def product(a_ref, b_ref):
        return (a_ref[...].astype(F32) * b_ref[...].astype(F32)).astype(BF16).astype(F32)

    def save(src, dst, n):
        copy = pltpu.make_async_copy(src, dst, save_sem.at[n])
        copy.start()
        return copy

    def finish(half, recv, left, right, results, first):
        saves = []
        block = width // 4
        count = block // part
        for n in (2 * half, 2 * half + 1):
            start = (n % 2) * count
            rows = unfold(recv[start : start + count])
            cols = slice(n * block, (n + 1) * block)
            direct = left[:, cols].astype(F32) * right[:, cols].astype(F32)
            direct = direct.astype(BF16).astype(F32)
            total = rows.reshape(block, span).T + skip_ref[:, cols] * direct
            for m, (factor, held, dst) in enumerate(results):
                held[:, cols] = (factor[:, cols].astype(F32) * total).astype(BF16)
                saves.append(save(held.at[:, cols], dst.at[:, cols], first + 2 * n + m))
        return saves

    loads = [
        pltpu.make_async_copy(src, dst, load_sem.at[n])
        for n, (src, dst) in enumerate(
            [
                (k_hbm, k_ref), (v_hbm, v_ref), (f_hbm, f_ref), (q_hbm, q_ref), (g_hbm, g_ref),
                (outer_fwd_hbm, outer_fwd), (twist_cos_hbm, twist_cos), (twist_sin_hbm, twist_sin),
                (inner_fwd_hbm, inner_fwd), (inner_inv_hbm, inner_inv), (outer_inv_hbm, outer_inv),
            ]
        )
    ]
    for load in loads:
        load.start()

    barrier = pltpu.get_barrier_semaphore()
    greet(barrier, lambda s: {"context": (me + s) % groups}, 1, groups)
    greet(barrier, lambda s: at_plane((1 - upper) * side + s), 0, side)
    pl.semaphore_signal(barrier, inc=1, device_id={"tensor": sibling}, device_id_type=MESH)
    loads[0].wait()
    loads[1].wait()
    x_send[...] = spread(product(k_ref, v_ref).T, groups)
    loads[2].wait()
    taps = f_ref[...].astype(F32)
    taps = jnp.where(first_core, taps[:, : width // 2], taps[:, width // 2 :]).T
    f_send[...] = fold(taps.reshape(groups, part, span))
    pl.semaphore_wait(barrier, groups + side)
    greet(ring_sem, lambda s: at_plane((1 - upper) * side + s), 0, side)
    start_some(x_send, x_recv, 0, 1, groups // 2)
    x_recv[pl.ds(me, 1)] = x_send[pl.ds(own, 1)]
    loads[3].wait()
    loads[4].wait()
    g_send[...] = spread(product(q_ref, g_ref).T, groups)
    for load in loads[5:]:
        load.wait()
    pl.semaphore_wait(ring_sem, side)
    start_nearest(f_send, f_recv, 1)
    start_some(x_send, x_recv, 0, groups // 2, groups)
    start_out(g_send, g_recv, 2)

    wait_all(f_recv, 1)
    swap = remote(f_recv, f_other, 3, {"tensor": sibling})
    swap.start()
    swap.wait()
    held, other = unfold(f_recv[...]), unfold(f_other[...])
    fill(
        jnp.concatenate(
            [jnp.where(first_core, held, other), jnp.where(first_core, other, held)], axis=1
        )
    )
    forward(spec_h)

    wait_all(x_recv, 0)
    fill(x_recv[...].astype(F32))
    mid = chans // step // 2
    forward(spec_x, 0, mid)
    inverse(spec_x, spec_h, False, 0, mid)
    c0_send[...] = packed(0).astype(BF16)
    start_home(c0_send, c0_recv, 4)
    forward(spec_x, mid, 2 * mid)
    inverse(spec_x, spec_h, False, mid, 2 * mid)
    c1_send[...] = packed(1).astype(BF16)
    start_home(c1_send, c1_recv, 10)

    wait_all(g_recv, 2)
    fill(g_recv[...].astype(F32))
    forward(spec_g)
    inverse(spec_x, spec_g, True)
    low, high = packed(0), packed(1)
    r_mine[...] = jnp.where(first_core, high, low).astype(BF16)
    swap = remote(r_mine, r_other, 5, {"tensor": sibling})
    swap.start()
    kept_buf[...] = jnp.where(first_core, low, high)

    inverse(spec_h, spec_g, True, 0, mid)
    b0_send[...] = packed(0).astype(BF16)
    swap.wait()
    total = kept_buf[...] + r_other[...].astype(F32)
    low, high = total[:, :part], total[:, part:]
    cut = (side, side, side, part, span // 2)
    sent = jnp.where(first_half, high, low).reshape(cut)
    kept = jnp.where(first_half, low, high).reshape(cut)
    partner = at_plane((1 - upper) * side + (mz + side // 2) % side)
    trades = []
    for h in range(2):
        for z in range(half):
            e_send[h][z] = sent[:, h * half + z].reshape(e_send[h].shape[1:]).astype(BF16)
            e_kept[h, z] = kept[:, h * half + z].reshape(e_send[h].shape[1:])
        trades.append(remote(e_send[h], e_recv[h], 12 + h, partner))
        trades[h].start()
    start_home(b0_send, b0_recv, 8)
    inverse(spec_h, spec_g, True, mid, 2 * mid)
    b1_send[...] = packed(1).astype(BF16)
    start_home(b1_send, b1_recv, 11)

    for h in range(2):
        trades[h].wait()
        total = e_kept[h] + e_recv[h][...].astype(F32)
        total = total.reshape(half, side * side, part, span // 2)
        for to in range(side * side):
            r_send[h][to] = jnp.concatenate([total[z, to] for z in range(half)], axis=0).astype(BF16)
        start_plane(r_send[h], r_mid[h], 6 + 8 * h)

    forth = [(q_ref, out_ref, out_hbm), (g_ref, dq_ref, dq_hbm)]
    back = [(v_ref, dk_ref, dk_hbm), (k_ref, dv_ref, dv_hbm)]
    wait_all(c0_recv, 4)
    saves = finish(0, c0_recv, k_ref, v_ref, forth, 0)
    for h in range(2):
        wait_all(r_mid[h], 6 + 8 * h)
        rows = r_mid[h][...].astype(F32)
        for z in range(half):
            level = rows[:, z * part : (z + 1) * part]
            s_send[h * half + z] = level.reshape(side * side * part, span // 2).astype(BF16)
        start_line(s_send, s_recv, 7, h * half)
    s_recv[pl.ds(level_of(mz, upper), 1)] = s_send[pl.ds(mz, 1)]
    wait_all(c1_recv, 10)
    saves += finish(1, c1_recv, k_ref, v_ref, forth, 0)
    wait_all(b0_recv, 8)
    saves += finish(0, b0_recv, q_ref, g_ref, back, 8)

    wait_all(s_recv, 7)
    some = [s_recv[z].astype(F32) for z in range(side)]
    run = side * part
    total = jnp.concatenate(
        [some[z][x * run : (x + 1) * run] for x in range(side) for z in range(side)], axis=0
    ).T
    quarter = span // 4
    t_send[...] = jnp.where(first_core, total[quarter:], total[:quarter])
    swap = remote(t_send, t_recv, 9, {"tensor": sibling})
    swap.start()
    own_buf[...] = jnp.where(first_core, total[:quarter], total[quarter:])
    wait_all(b1_recv, 11)
    saves += finish(1, b1_recv, q_ref, g_ref, back, 8)
    swap.wait()
    held, other = own_buf[...], t_recv[...]
    df_ref[:, : width // 2] = jnp.where(first_core, held, other)
    df_ref[:, width // 2 :] = jnp.where(first_core, other, held)
    saves.append(save(df_ref, df_hbm, 16))
    for copy in saves:
        copy.wait()


def hand_over(*refs):
    load_sem, save_sem = refs[15:]
    loads, saves = [], []
    for n in range(5):
        src, dst, held = refs[n], refs[5 + n], refs[10 + n]
        part = src.shape[0] // 2
        for m in range(2):
            rows = pl.ds(m * part, part)
            loads.append(pltpu.make_async_copy(src.at[rows], held.at[rows], load_sem.at[n, m]))
            saves.append(pltpu.make_async_copy(held.at[rows], dst.at[rows], save_sem.at[n, m]))
    for load in loads:
        load.start()
    for load, copy in zip(loads, saves):
        load.wait()
        copy.start()
    for copy in saves:
        copy.wait()


def shards(queries, keys, values, cotangent, filter_param, skip):
    span, width = queries.shape
    groups = lax.axis_size("context")
    side = round(groups ** (1 / 3))
    chans = width // groups
    part = chans // 2
    length = groups * span
    scale = 1.0 / (length * math.sqrt(length))
    tables = make_tables(groups, span)
    whole = pl.BlockSpec(memory_space=pltpu.VMEM)
    anywhere = pl.BlockSpec(memory_space=pl.ANY)
    wide = pltpu.VMEM((span, width), BF16)
    big = pltpu.VMEM((groups, chans, span), BF16)
    small = pltpu.VMEM((groups, chans, span // 2), BF16)
    rows = pltpu.VMEM((side // 2, side * side * part, span // 2), BF16)
    chunk = pltpu.VMEM((side * side, side // 2 * part, span // 2), BF16)
    line = pltpu.VMEM((side, side * side * part, span // 2), BF16)
    shape = jax.ShapeDtypeStruct((span, width), BF16)
    shapes = (shape,) * 4 + (jax.ShapeDtypeStruct((span // 4, width), F32),)
    results = pl.pallas_call(
        functools.partial(kernel, groups, side, scale),
        out_shape=shapes,
        in_specs=[anywhere] * 5 + [whole] + [anywhere] * 6,
        out_specs=(anywhere,) * 5,
        scratch_shapes=[wide] * 5
        + [pltpu.VMEM(t.shape, t.dtype) for t in tables]
        + [big] * 4
        + [small] * 13
        + [
            rows,
            rows,
            rows,
            rows,
            pltpu.VMEM((2, side // 2, side * side * part, span // 2), F32),
            chunk,
            chunk,
            chunk,
            chunk,
            line,
            line,
        ]
        + [pltpu.VMEM((span // 4, width // 2), F32)] * 3
        + [pltpu.VMEM((2, groups * chans, span // 2), F32)]
        + [pltpu.VMEM((groups, chans, span // 2), F32)]
        + [pltpu.VMEM((groups * chans, 2 * span), F32)] * 3
        + [wide] * 4
        + [pltpu.VMEM((span // 4, width), F32)]
        + [pltpu.SemaphoreType.DMA((17,)), pltpu.SemaphoreType.DMA((11,))]
        + [pltpu.SemaphoreType.DMA((15,))] * 2
        + [pltpu.SemaphoreType.REGULAR],
        compiler_params=pltpu.CompilerParams(
            collective_id=0, has_side_effects=True, vmem_limit_bytes=56 * 1024 * 1024
        ),
    )(queries, keys, values, cotangent, filter_param, skip.reshape(1, width), *tables)
    return pl.pallas_call(
        hand_over,
        out_shape=shapes,
        in_specs=[anywhere] * 5,
        out_specs=(anywhere,) * 5,
        scratch_shapes=[pltpu.VMEM(r.shape, r.dtype) for r in shapes]
        + [pltpu.SemaphoreType.DMA((5, 2))] * 2,
    )(*results)


def solution(mesh):
    placed = (
        P("context", "tensor"),
        P("context", "tensor"),
        P("context", "tensor"),
        P("context", "tensor"),
        P("context", None),
        P("tensor"),
    )
    return jax.shard_map(
        shards,
        mesh=mesh,
        in_specs=placed,
        out_specs=(
            P("context", "tensor"),
            P("context", "tensor"),
            P("context", "tensor"),
            P("context", "tensor"),
            P(("context", "tensor"), None),
        ),
        check_vma=False,
    )
```

```python
import functools
import math

import jax
import jax.numpy as jnp
import ml_dtypes
import numpy as np
from jax import lax
from jax.experimental import pallas as pl
from jax.experimental.pallas import tpu as pltpu
from jax.sharding import PartitionSpec as P

MESH = pl.DeviceIdType.MESH
F32 = jnp.float32
BF16 = jnp.bfloat16


def make_tables(blocks, span):
    length = blocks * span
    row = np.arange(blocks, dtype=np.float64)
    col = np.arange(span, dtype=np.float64)
    outer = 2.0 * np.pi * np.outer(row + 0.25, row) / blocks
    twist = 2.0 * np.pi * np.outer(row + 0.25, col) / length
    inner = 2.0 * np.pi * (np.outer(col, col) % span) / span
    outer_fwd = np.concatenate([np.cos(outer), -np.sin(outer)], axis=0)
    outer_inv = np.concatenate([np.cos(outer).T, -np.sin(outer).T], axis=1)
    cos, sin = np.cos(inner), np.sin(inner)
    inner_fwd = np.block([[cos, -sin], [sin, cos]])
    inner_inv = np.block([[cos, sin], [-sin, cos]])
    half = ml_dtypes.bfloat16
    return (
        outer_fwd.astype(half),
        outer_inv.astype(half),
        np.cos(twist).astype(np.float32),
        (-np.sin(twist)).astype(np.float32),
        inner_fwd.astype(half),
        inner_inv.astype(half),
    )


def dot(a, b):
    return jnp.dot(a, b, preferred_element_type=F32)


def spread(turned, groups):
    rows, span = turned.shape
    part = rows // (2 * groups)
    first = turned[: rows // 2].reshape(groups, part, span)
    second = turned[rows // 2 :].reshape(groups, part, span)
    return jnp.concatenate([first, second], axis=1).astype(BF16)


def fold(rows):
    half = rows.shape[2] // 2
    return jnp.concatenate([rows[:, :, :half], rows[:, :, half:]], axis=1).astype(BF16)


def unfold(rows):
    part = rows.shape[1] // 2
    wide = rows.astype(F32)
    return jnp.concatenate([wide[:, :part], wide[:, part:]], axis=2)


def kernel(
    groups,
    side,
    scale,
    q_hbm, k_hbm, v_hbm, g_hbm, f_hbm, skip_ref,
    outer_fwd_hbm, outer_inv_hbm, twist_cos_hbm, twist_sin_hbm, inner_fwd_hbm, inner_inv_hbm,
    out_hbm, dq_hbm, dk_hbm, dv_hbm, df_hbm,
    q_ref, k_ref, v_ref, g_ref, f_ref,
    outer_fwd, outer_inv, twist_cos, twist_sin, inner_fwd, inner_inv,
    x_send, x_recv, g_send, g_recv,
    c0_send, c0_recv, c1_send, c1_recv, b0_send, b0_recv, b1_send, b1_recv,
    f_send, f_recv, f_other, r_mine, r_other,
    e0_send, e1_send, e0_recv, e1_recv, e_kept, r0_send, r1_send, r0_mid, r1_mid, s_send, s_recv, t_send, t_recv, own_buf,
    time_buf, kept_buf, spec_x, spec_h, spec_g,
    out_ref, dq_ref, dk_ref, dv_ref, df_ref,
    save_sem, load_sem, send_sem, recv_sem, ring_sem,
):
    e_send, e_recv = (e0_send, e1_send), (e0_recv, e1_recv)
    r_send, r_mid = (r0_send, r1_send), (r0_mid, r1_mid)
    span, width = q_ref.shape
    chans = x_send.shape[1]
    part = chans // 2
    half = side // 2
    step = min(4, chans)
    me = lax.axis_index("context")
    mine = lax.axis_index("tensor")
    core = mine % 2
    upper = mine // 2
    sibling = mine + 1 - 2 * core
    mx, mz, my = me // (side * side), (me // side) % side, me % side
    place = mx * side + my
    near = (mz // (side // 2) + upper) % 2
    first_core = core == 0
    first_half = upper == 0

    def level_of(z, up):
        return (z + up * (side // 2)) % side

    def group_of(to, up):
        x, z, y = to // (side * side), (to // side) % side, to % side
        return (x * side + level_of(z, up)) * side + y

    own = group_of(me, upper)

    def at_place(s):
        x, y = s // side, s % side
        return {"context": (x * side + mz) * side + y}

    def at_plane(p):
        return {"context": (mx * side + p % side) * side + my, "tensor": (p // side) * 2 + core}

    def greet(sem, where, first, count):
        def body(s, carry):
            pl.semaphore_signal(sem, inc=1, device_id=where(s), device_id_type=MESH)
            return carry
        lax.fori_loop(first, count, body, 0)

    def remote(src, dst, slot, where):
        return pltpu.make_async_remote_copy(
            src_ref=src, dst_ref=dst,
            send_sem=send_sem.at[slot], recv_sem=recv_sem.at[slot],
            device_id=where, device_id_type=MESH,
        )

    def start_some(src, dst, slot, first, last):
        def body(s, carry):
            to = (me + s) % groups
            remote(src.at[group_of(to, upper)], dst.at[me], slot, {"context": to}).start()
            return carry
        lax.fori_loop(first, last, body, 0)

    def start_out(src, dst, slot):
        start_some(src, dst, slot, 1, groups)
        dst[pl.ds(me, 1)] = src[pl.ds(own, 1)]

    def start_home(src, dst, slot):
        def body(s, carry):
            to = (me + s) % groups
            remote(src.at[to], dst.at[own], slot, {"context": to}).start()
            return carry
        lax.fori_loop(1, groups, body, 0)
        dst[pl.ds(own, 1)] = src[pl.ds(me, 1)]

    def start_nearest(src, dst, slot):
        def body(s, carry):
            to = (me + s) % groups
            up = (near + ((to // side) % side) // (side // 2)) % 2
            where = {"context": to, "tensor": 2 * up + core}
            remote(src.at[group_of(to, up)], dst.at[me], slot, where).start()
            return carry
        lax.fori_loop(1, groups, body, 0)
        dst[pl.ds(me, 1)] = src[pl.ds(own, 1)]

    def start_plane(src, dst, slot):
        def body(s, carry):
            to = (place + s) % (side * side)
            remote(src.at[to], dst.at[place], slot, at_place(to)).start()
            return carry
        lax.fori_loop(1, side * side, body, 0)
        dst[pl.ds(place, 1)] = src[pl.ds(place, 1)]

    def start_line(src, dst, slot, first):
        def body(s, carry):
            to = first + s

            @pl.when(to != mz)
            def _():
                where = at_plane(upper * side + to)
                remote(src.at[to], dst.at[level_of(mz, upper)], slot, where).start()

            return carry
        lax.fori_loop(0, side // 2, body, 0)

    def wait_all(dst, slot):
        blocks = dst.at[pl.ds(0, dst.shape[0] - 1)]
        remote(blocks, blocks, slot, {"tensor": sibling}).wait()

    def fill(field):
        flat = field.reshape(groups * chans, span)
        time_buf[0] = flat[:, : span // 2]
        time_buf[1] = flat[:, span // 2 :]

    def packed(n):
        low = time_buf[0].reshape(groups, chans, span // 2)[:, n * part : (n + 1) * part]
        high = time_buf[1].reshape(groups, chans, span // 2)[:, n * part : (n + 1) * part]
        return jnp.concatenate([low, high], axis=1)

    def forward(dst, first=0, last=chans // step):
        def body(n, carry):
            parts = []
            for c in range(step):
                rows = pl.ds(n * step + c, groups, stride=chans)
                field = jnp.concatenate([time_buf[0, rows, :], time_buf[1, rows, :]], axis=1)
                first = dot(outer_fwd[...], field.astype(BF16))
                re, im = first[:groups], first[groups:]
                tc, ts = twist_cos[...], twist_sin[...]
                parts.append(
                    jnp.concatenate([re * tc - im * ts, re * ts + im * tc], axis=1).astype(BF16)
                )
            rows = jnp.concatenate(parts, axis=0)
            here = pl.ds(pl.multiple_of(n * step * groups, step * groups), step * groups)
            dst[here, :] = dot(rows, inner_fwd[...])
            return carry
        lax.fori_loop(first, last, body, 0)

    def inverse(a_ref, b_ref, conj, first=0, last=chans // step):
        def body(n, carry):
            here = pl.ds(pl.multiple_of(n * step * groups, step * groups), step * groups)
            ar, ai = a_ref[here, :span], a_ref[here, span:]
            br, bi = b_ref[here, :span], b_ref[here, span:]
            if conj:
                re, im = ar * br + ai * bi, ar * bi - ai * br
            else:
                re, im = ar * br - ai * bi, ar * bi + ai * br
            prod = jnp.concatenate([re, im], axis=1).astype(BF16)
            back = dot(prod, inner_inv[...])
            tc, ts = twist_cos[...], twist_sin[...]
            for c in range(step):
                re = back[c * groups : (c + 1) * groups, :span]
                im = back[c * groups : (c + 1) * groups, span:]
                both = jnp.concatenate([re * tc + im * ts, im * tc - re * ts], axis=0)
                field = dot(outer_inv[...], both.astype(BF16)) * scale
                rows = pl.ds(n * step + c, groups, stride=chans)
                time_buf[0, rows, :] = field[:, : span // 2]
                time_buf[1, rows, :] = field[:, span // 2 :]
            return carry
        lax.fori_loop(first, last, body, 0)

    def product(a_ref, b_ref):
        return (a_ref[...].astype(F32) * b_ref[...].astype(F32)).astype(BF16).astype(F32)

    def save(src, dst, n):
        copy = pltpu.make_async_copy(src, dst, save_sem.at[n])
        copy.start()
        return copy

    def finish(half, recv, left, right, results, first):
        saves = []
        block = width // 4
        count = block // part
        for n in (2 * half, 2 * half + 1):
            start = (n % 2) * count
            rows = unfold(recv[start : start + count])
            cols = slice(n * block, (n + 1) * block)
            direct = left[:, cols].astype(F32) * right[:, cols].astype(F32)
            direct = direct.astype(BF16).astype(F32)
            total = rows.reshape(block, span).T + skip_ref[:, cols] * direct
            for m, (factor, held, dst) in enumerate(results):
                held[:, cols] = (factor[:, cols].astype(F32) * total).astype(BF16)
                saves.append(save(held.at[:, cols], dst.at[:, cols], first + 2 * n + m))
        return saves

    loads = [
        pltpu.make_async_copy(src, dst, load_sem.at[n])
        for n, (src, dst) in enumerate(
            [
                (k_hbm, k_ref), (v_hbm, v_ref), (f_hbm, f_ref), (q_hbm, q_ref), (g_hbm, g_ref),
                (outer_fwd_hbm, outer_fwd), (twist_cos_hbm, twist_cos), (twist_sin_hbm, twist_sin),
                (inner_fwd_hbm, inner_fwd), (inner_inv_hbm, inner_inv), (outer_inv_hbm, outer_inv),
            ]
        )
    ]
    for load in loads:
        load.start()

    barrier = pltpu.get_barrier_semaphore()
    greet(barrier, lambda s: {"context": (me + s) % groups}, 1, groups)
    greet(barrier, lambda s: at_plane((1 - upper) * side + s), 0, side)
    pl.semaphore_signal(barrier, inc=1, device_id={"tensor": sibling}, device_id_type=MESH)
    loads[0].wait()
    loads[1].wait()
    x_send[...] = spread(product(k_ref, v_ref).T, groups)
    loads[2].wait()
    taps = f_ref[...].astype(F32)
    taps = jnp.where(first_core, taps[:, : width // 2], taps[:, width // 2 :]).T
    f_send[...] = fold(taps.reshape(groups, part, span))
    pl.semaphore_wait(barrier, groups + side)
    greet(ring_sem, lambda s: at_plane((1 - upper) * side + s), 0, side)
    start_some(x_send, x_recv, 0, 1, groups // 2)
    x_recv[pl.ds(me, 1)] = x_send[pl.ds(own, 1)]
    loads[3].wait()
    loads[4].wait()
    g_send[...] = spread(product(q_ref, g_ref).T, groups)
    for load in loads[5:]:
        load.wait()
    pl.semaphore_wait(ring_sem, side)
    start_nearest(f_send, f_recv, 1)
    start_some(x_send, x_recv, 0, groups // 2, groups)
    start_out(g_send, g_recv, 2)

    wait_all(f_recv, 1)
    swap = remote(f_recv, f_other, 3, {"tensor": sibling})
    swap.start()
    swap.wait()
    held, other = unfold(f_recv[...]), unfold(f_other[...])
    fill(
        jnp.concatenate(
            [jnp.where(first_core, held, other), jnp.where(first_core, other, held)], axis=1
        )
    )
    forward(spec_h)

    wait_all(x_recv, 0)
    fill(x_recv[...].astype(F32))
    mid = chans // step // 2
    forward(spec_x, 0, mid)
    inverse(spec_x, spec_h, False, 0, mid)
    c0_send[...] = packed(0).astype(BF16)
    start_home(c0_send, c0_recv, 4)
    forward(spec_x, mid, 2 * mid)
    inverse(spec_x, spec_h, False, mid, 2 * mid)
    c1_send[...] = packed(1).astype(BF16)
    start_home(c1_send, c1_recv, 10)

    wait_all(g_recv, 2)
    fill(g_recv[...].astype(F32))
    forward(spec_g)
    inverse(spec_x, spec_g, True)
    low, high = packed(0), packed(1)
    r_mine[...] = jnp.where(first_core, high, low).astype(BF16)
    swap = remote(r_mine, r_other, 5, {"tensor": sibling})
    swap.start()
    kept_buf[...] = jnp.where(first_core, low, high)

    inverse(spec_h, spec_g, True, 0, mid)
    b0_send[...] = packed(0).astype(BF16)
    swap.wait()
    total = kept_buf[...] + r_other[...].astype(F32)
    low, high = total[:, :part], total[:, part:]
    cut = (side, side, side, part, span // 2)
    sent = jnp.where(first_half, high, low).reshape(cut)
    kept = jnp.where(first_half, low, high).reshape(cut)
    partner = at_plane((1 - upper) * side + (mz + side // 2) % side)
    trades = []
    for h in range(2):
        for z in range(half):
            e_send[h][z] = sent[:, h * half + z].reshape(e_send[h].shape[1:]).astype(BF16)
            e_kept[h, z] = kept[:, h * half + z].reshape(e_send[h].shape[1:])
        trades.append(remote(e_send[h], e_recv[h], 12 + h, partner))
        trades[h].start()
    start_home(b0_send, b0_recv, 8)
    inverse(spec_h, spec_g, True, mid, 2 * mid)
    b1_send[...] = packed(1).astype(BF16)
    start_home(b1_send, b1_recv, 11)

    for h in range(2):
        trades[h].wait()
        total = e_kept[h] + e_recv[h][...].astype(F32)
        total = total.reshape(half, side * side, part, span // 2)
        for to in range(side * side):
            r_send[h][to] = jnp.concatenate([total[z, to] for z in range(half)], axis=0).astype(BF16)
        start_plane(r_send[h], r_mid[h], 6 + 8 * h)

    forth = [(q_ref, out_ref, out_hbm), (g_ref, dq_ref, dq_hbm)]
    back = [(v_ref, dk_ref, dk_hbm), (k_ref, dv_ref, dv_hbm)]
    for h in range(2):
        wait_all(r_mid[h], 6 + 8 * h)
        rows = r_mid[h][...].astype(F32)
        for z in range(half):
            level = rows[:, z * part : (z + 1) * part]
            s_send[h * half + z] = level.reshape(side * side * part, span // 2).astype(BF16)
        start_line(s_send, s_recv, 7, h * half)
    s_recv[pl.ds(level_of(mz, upper), 1)] = s_send[pl.ds(mz, 1)]
    wait_all(c0_recv, 4)
    saves = finish(0, c0_recv, k_ref, v_ref, forth, 0)
    wait_all(c1_recv, 10)
    saves += finish(1, c1_recv, k_ref, v_ref, forth, 0)
    wait_all(b0_recv, 8)
    saves += finish(0, b0_recv, q_ref, g_ref, back, 8)

    wait_all(s_recv, 7)
    some = [s_recv[z].astype(F32) for z in range(side)]
    run = side * part
    total = jnp.concatenate(
        [some[z][x * run : (x + 1) * run] for x in range(side) for z in range(side)], axis=0
    ).T
    quarter = span // 4
    t_send[...] = jnp.where(first_core, total[quarter:], total[:quarter])
    swap = remote(t_send, t_recv, 9, {"tensor": sibling})
    swap.start()
    own_buf[...] = jnp.where(first_core, total[:quarter], total[quarter:])
    wait_all(b1_recv, 11)
    saves += finish(1, b1_recv, q_ref, g_ref, back, 8)
    swap.wait()
    held, other = own_buf[...], t_recv[...]
    df_ref[:, : width // 2] = jnp.where(first_core, held, other)
    df_ref[:, width // 2 :] = jnp.where(first_core, other, held)
    saves.append(save(df_ref, df_hbm, 16))
    for copy in saves:
        copy.wait()


def hand_over(*refs):
    load_sem, save_sem = refs[15:]
    loads, saves = [], []
    for n in range(5):
        src, dst, held = refs[n], refs[5 + n], refs[10 + n]
        part = src.shape[0] // 2
        for m in range(2):
            rows = pl.ds(m * part, part)
            loads.append(pltpu.make_async_copy(src.at[rows], held.at[rows], load_sem.at[n, m]))
            saves.append(pltpu.make_async_copy(held.at[rows], dst.at[rows], save_sem.at[n, m]))
    for load in loads:
        load.start()
    for load, copy in zip(loads, saves):
        load.wait()
        copy.start()
    for copy in saves:
        copy.wait()


def shards(queries, keys, values, cotangent, filter_param, skip):
    span, width = queries.shape
    groups = lax.axis_size("context")
    side = round(groups ** (1 / 3))
    chans = width // groups
    part = chans // 2
    length = groups * span
    scale = 1.0 / (length * math.sqrt(length))
    tables = make_tables(groups, span)
    whole = pl.BlockSpec(memory_space=pltpu.VMEM)
    anywhere = pl.BlockSpec(memory_space=pl.ANY)
    wide = pltpu.VMEM((span, width), BF16)
    big = pltpu.VMEM((groups, chans, span), BF16)
    small = pltpu.VMEM((groups, chans, span // 2), BF16)
    rows = pltpu.VMEM((side // 2, side * side * part, span // 2), BF16)
    chunk = pltpu.VMEM((side * side, side // 2 * part, span // 2), BF16)
    line = pltpu.VMEM((side, side * side * part, span // 2), BF16)
    shape = jax.ShapeDtypeStruct((span, width), BF16)
    shapes = (shape,) * 4 + (jax.ShapeDtypeStruct((span // 4, width), F32),)
    results = pl.pallas_call(
        functools.partial(kernel, groups, side, scale),
        out_shape=shapes,
        in_specs=[anywhere] * 5 + [whole] + [anywhere] * 6,
        out_specs=(anywhere,) * 5,
        scratch_shapes=[wide] * 5
        + [pltpu.VMEM(t.shape, t.dtype) for t in tables]
        + [big] * 4
        + [small] * 13
        + [
            rows,
            rows,
            rows,
            rows,
            pltpu.VMEM((2, side // 2, side * side * part, span // 2), F32),
            chunk,
            chunk,
            chunk,
            chunk,
            line,
            line,
        ]
        + [pltpu.VMEM((span // 4, width // 2), F32)] * 3
        + [pltpu.VMEM((2, groups * chans, span // 2), F32)]
        + [pltpu.VMEM((groups, chans, span // 2), F32)]
        + [pltpu.VMEM((groups * chans, 2 * span), F32)] * 3
        + [wide] * 4
        + [pltpu.VMEM((span // 4, width), F32)]
        + [pltpu.SemaphoreType.DMA((17,)), pltpu.SemaphoreType.DMA((11,))]
        + [pltpu.SemaphoreType.DMA((15,))] * 2
        + [pltpu.SemaphoreType.REGULAR],
        compiler_params=pltpu.CompilerParams(
            collective_id=0, has_side_effects=True, vmem_limit_bytes=56 * 1024 * 1024
        ),
    )(queries, keys, values, cotangent, filter_param, skip.reshape(1, width), *tables)
    return pl.pallas_call(
        hand_over,
        out_shape=shapes,
        in_specs=[anywhere] * 5,
        out_specs=(anywhere,) * 5,
        scratch_shapes=[pltpu.VMEM(r.shape, r.dtype) for r in shapes]
        + [pltpu.SemaphoreType.DMA((5, 2))] * 2,
    )(*results)


def solution(mesh):
    placed = (
        P("context", "tensor"),
        P("context", "tensor"),
        P("context", "tensor"),
        P("context", "tensor"),
        P("context", None),
        P("tensor"),
    )
    return jax.shard_map(
        shards,
        mesh=mesh,
        in_specs=placed,
        out_specs=(
            P("context", "tensor"),
            P("context", "tensor"),
            P("context", "tensor"),
            P("context", "tensor"),
            P(("context", "tensor"), None),
        ),
        check_vma=False,
    )
```
